128 devices in a mesh: gx: 16 (over x, y), gy: 8 (over z, core).
Axes of the slice: x: 4, y: 4, z: 4, core: 2. Of those that a mesh axis runs over, the one named last changes fastest.
Arguments:
- volume: bfloat16 [26, 512, 4096], P(None, 'gx', 'gy'), may hold values from -6 to 6
- owner: int32 [16, 8, 32, 1], P('gx', 'gy'), may hold values from 0 to 127; in each aligned block of 32 rows (0 to 31, 32 to 63, ..., all dimensions but the last counted through in order) at most 2 rows name the same one
- flags: int32 [16, 8, 32], P('gx', 'gy'), may hold values 0 or 1
Outputs:
- geometry: float32 [7, 4, 128, 1024], P(None, None, 'gx', 'gy')
- received: float32 [128, 256, 7, 128], P(('gx', 'gy'))
The draws below stay inside these ranges and needn't reach their ends.
Inputs may be any that keep to these rules, and one draw needn't show every extreme that they name: Within the rows of one device, at most 2 name the same owner, and in every draw some owner is named by exactly 2 rows of some device.
All inputs are finite; a program needn't handle non-finite values. No bound on the sum of `flags` on one device may be relied on, other than what follows from the above.
Results may differ from the reference program's by a relative error of at most 0.0003.
Values may be sent and summed in bfloat16 or wider, within the bound.
A program may use at most 128 MiB of HBM per device.

```python
import math
import jax
import jax.numpy as jnp
import numpy as np
from jax import lax

PLANES = 16
ROW = 128
LAYERS = 4
XF = 8
ROWS_DEV = 32
CAP = 2
NX = 512
NY = 4096
N_GX = 16
N_GY = 8
DEVICES = 128


def with_ends(array, stream_key, least, top_value):
    dims = array.shape
    place = [jax.random.randint(jax.random.fold_in(stream_key, axis), (), 0, dims[axis]) for axis in range(len(dims))]
    array = array.at[tuple(place)].set(least)
    longest = dims.index(max(dims))
    place[longest] = (place[longest] + 1) % dims[longest]
    return array.at[tuple(place)].set(top_value)


def block_scale(rng, shape, shards, low, top_value):
    loudness, own = 1.0, jax.random.fold_in(rng, 6)
    for axis_at, blocks in shards:
        steps = jnp.exp(jax.random.uniform(jax.random.fold_in(own, axis_at), (blocks,), jnp.float32, low / len(shards), top_value / len(shards)))
        loudness = loudness * jnp.repeat(steps, shape[axis_at] // blocks).reshape([-1 if axis == axis_at else 1 for axis in range(len(shape))])
    return loudness


def routed_block(stream_key, own, number, rows, number_of, top, most, skew):
    order = jax.random.permutation(stream_key, number_of)
    crowded, ordinary = shares(number_of, rows * top, most, skew, True), shares(number_of, rows * top, most, skew, False)
    places = jnp.arange(number_of)

    def named(sizes, turn):
        used = int((sizes > 0).sum())
        fixed = max(1, used // 4)
        moved = fixed + (places - fixed + turn * (used - fixed)) % max(1, number_of - fixed)
        return jnp.zeros((number_of,), jnp.int32).at[order[jnp.where(places < fixed, places, moved)]].set(jnp.asarray(sizes, jnp.int32))

    sizes = jnp.where(number % 4 == 0, named(crowded, number // 4), named(ordinary, number - number // 4 - 1))
    mixed = jax.random.permutation(jax.random.fold_in(own, 3), number_of)
    giver, receiver = mixed[0:number_of // 2 * 2:2], mixed[1:number_of // 2 * 2:2]
    margin = jnp.minimum(sizes[giver] - 1, most - sizes[receiver]) // 2
    margin = jnp.where((giver == order[0]) | (receiver == order[0]) | (sizes[receiver] == 0), 0, jnp.maximum(margin, 0))
    moved = jax.random.randint(jax.random.fold_in(own, 4), (number_of // 2,), 0, 1 << 20) % (margin + 1)
    sizes = sizes.at[giver].add(-moved).at[receiver].add(moved)
    items = jnp.searchsorted(jnp.cumsum(sizes), jnp.arange(rows * top), side="right").astype(jnp.int32)
    table = items.reshape(top, rows).T
    table = table[jax.random.permutation(jax.random.fold_in(own, 1), rows)]
    turn = jax.random.randint(jax.random.fold_in(own, 2), (rows, 1), 0, top)
    return jnp.take_along_axis(table, (jnp.arange(top)[None, :] + turn) % top, axis=1)


def shares(number_of, total, limit, slope, full):
    weights = [(1 << 20) // math.isqrt(grade ** slope) + 1 for grade in range(1, number_of + 1)]
    largest = limit if full else min(limit, max(-(-total // number_of), total * weights[0] // sum(weights)))
    least = 1 if total - largest >= number_of - 1 else 0
    counts, rest = [largest] + [least] * (number_of - 1), total - largest - least * (number_of - 1)
    while rest > 0:
        candidates = [i for i in range(1, number_of) if counts[i] < largest] or [i for i in range(1, number_of) if counts[i] < limit]
        mass, remaining = sum([weights[i] for i in candidates]), rest
        for i in candidates:
            extra = min(limit - counts[i], max(1, remaining * weights[i] // mass), rest)
            counts[i] = counts[i] + extra
            rest = rest - extra
    return np.array(counts)


def scatter_about(own_key, shape, width, bound, cuts=(), held_as=jnp.bfloat16):
    loudness = block_scale(own_key, shape, cuts, -0.22, 0.18) if cuts else 1.0
    values = jax.random.normal(own_key, shape, jnp.float32) * width * loudness
    return jnp.minimum(jnp.maximum(values, -bound), bound).astype(held_as)


def setup_inputs(seed: int = 0) -> dict:
    arg_keys = jax.random.split(jax.random.key(seed), 4)
    volume = scatter_about(arg_keys[0], (PLANES + 10, NX, NY), 1.0, 6.0, ((1, 16), (2, 8)))
    owner_keys = jax.random.split(jax.random.fold_in(arg_keys[1], 1), N_GX * N_GY * ROWS_DEV // ROWS_DEV)
    owner_turns = jax.random.permutation(jax.random.fold_in(arg_keys[1], 3), N_GX * N_GY * ROWS_DEV // ROWS_DEV)
    owner = jax.vmap(lambda own, number: routed_block(jax.random.fold_in(arg_keys[1], 2), own, number, ROWS_DEV, DEVICES, 1, CAP, 2))(owner_keys, owner_turns).reshape((N_GX, N_GY, ROWS_DEV, 1))
    flags = with_ends((jax.random.randint(arg_keys[2], (N_GX, N_GY, ROWS_DEV), 0, 8) < 7).astype(jnp.int32), jax.random.fold_in(arg_keys[2], 1), 0, 1)
    return {"volume": volume, "owner": owner, "flags": flags}


raw_taps = [math.exp(-(offset - 4) ** 2 / 8.0) for offset in range(9)]
gauss_taps = [value / sum(raw_taps) for value in raw_taps]
sharpness = 20.0
normal_floor = 0.01

def smooth_valid(padded):
    planes = padded.shape[0] - 8
    along_z = gauss_taps[0] * padded[0:planes].astype(jnp.float32)
    for offset in range(1, 9):
        along_z = along_z + gauss_taps[offset] * padded[offset:offset + planes].astype(jnp.float32)
    width_x = padded.shape[1] - 8
    along_x = gauss_taps[0] * along_z[:, 0:width_x]
    for offset in range(1, 9):
        along_x = along_x + gauss_taps[offset] * along_z[:, offset:offset + width_x]
    width_y = padded.shape[2] - 8
    along_y = gauss_taps[0] * along_x[:, :, 0:width_y]
    for offset in range(1, 9):
        along_y = along_y + gauss_taps[offset] * along_x[:, :, offset:offset + width_y]
    return along_y

def pair_smooth(field, axis):
    length = field.shape[axis] - 2
    lower = lax.slice_in_dim(field, 0, length, axis=axis)
    middle = lax.slice_in_dim(field, 1, length + 1, axis=axis)
    upper = lax.slice_in_dim(field, 2, length + 2, axis=axis)
    return 0.25 * lower + 0.5 * middle + 0.25 * upper

def pair_slope(field, axis):
    length = field.shape[axis] - 2
    lower = lax.slice_in_dim(field, 0, length, axis=axis)
    upper = lax.slice_in_dim(field, 2, length + 2, axis=axis)
    return 0.5 * (upper - lower)

def features(indicator, layers):
    blur_z = pair_smooth(indicator, 0)
    slope_z = pair_slope(indicator, 0)
    grad_z = pair_smooth(pair_smooth(slope_z, 1), 2)
    grad_x = pair_smooth(pair_slope(blur_z, 1), 2)
    grad_y = pair_slope(pair_smooth(blur_z, 1), 2)
    inner = indicator[1:-1, 1:-1, 1:-1]
    cells_x = inner.shape[1] // 4
    cells_y = inner.shape[2] // 4

    def blocks(field):
        return field.reshape(layers, 4, cells_x, 4, cells_y, 4)
    inner_blocks = blocks(inner)
    fraction = lax.optimization_barrier(jnp.mean(inner_blocks, axis=(1, 3, 5)))
    aperture_z = lax.optimization_barrier(jnp.mean(inner_blocks[:, 0], axis=(2, 4)))
    aperture_x = lax.optimization_barrier(jnp.mean(inner_blocks[:, :, :, 0], axis=(1, 4)))
    aperture_y = lax.optimization_barrier(jnp.mean(inner_blocks[..., 0], axis=(1, 3)))
    mean_z = lax.optimization_barrier(jnp.mean(blocks(grad_z), axis=(1, 3, 5)))
    mean_x = lax.optimization_barrier(jnp.mean(blocks(grad_x), axis=(1, 3, 5)))
    mean_y = lax.optimization_barrier(jnp.mean(blocks(grad_y), axis=(1, 3, 5)))
    length = jnp.sqrt(mean_z * mean_z + mean_x * mean_x + mean_y * mean_y + normal_floor)
    return jnp.stack([fraction, aperture_z, aperture_x, aperture_y, -mean_z / length, -mean_x / length, -mean_y / length])

def reference(volume, owner, flags):
    layers = PLANES // 4
    pieces = []
    for layer in range(layers):
        block = volume[4 * layer:4 * layer + 14]
        padded = jnp.pad(block, ((0, 0), (4, 4), (4, 4)))
        indicator = jax.nn.sigmoid(sharpness * smooth_valid(padded))
        indicator = jnp.pad(indicator, ((0, 0), (1, 1), (1, 1)))
        pieces.append(features(indicator, 1))
    geometry = jnp.concatenate(pieces, axis=1)
    device_count = N_GX * N_GY
    row_count = LAYERS * XF
    rows_all = geometry.reshape(7, LAYERS, N_GX, XF, N_GY, ROW)
    rows_all = jnp.transpose(rows_all, (2, 4, 1, 3, 0, 5)).reshape(device_count, row_count, 7, ROW)
    owners_all = owner.reshape(device_count, row_count)
    flags_all = flags.reshape(device_count, row_count)
    targets = jnp.arange(device_count, dtype=jnp.int32)
    chosen = ((owners_all[:, :, None] == targets[None, None, :]) & (flags_all[:, :, None] == 1)).astype(jnp.int32)
    before = jnp.cumsum(chosen, axis=1) - chosen
    slots = lax.optimization_barrier(jnp.sum(before * chosen, axis=2))
    source = jnp.arange(device_count, dtype=jnp.int32)[:, None]
    dump = device_count * device_count * CAP
    target = jnp.where(flags_all == 1, owners_all * (device_count * CAP) + source * CAP + slots, dump)
    buffer = jnp.zeros((dump + 1, 7, ROW), jnp.float32)
    buffer = buffer.at[target.reshape(-1)].set(rows_all.reshape(-1, 7, ROW))
    received = buffer[:-1].reshape(device_count, device_count * CAP, 7, ROW)
    return (geometry, received)
```

```python
import functools
import math

import jax
import jax.numpy as jnp
from jax import lax
from jax.experimental import pallas as pl
from jax.experimental.pallas import tpu as pltpu
from jax.sharding import PartitionSpec as P

raw_taps = [math.exp(-((offset - 4) ** 2) / 8.0) for offset in range(9)]
gauss_taps = [value / sum(raw_taps) for value in raw_taps]
sharpness = 20.0
normal_floor = 0.01


def with_halo(block, sides, width):
    for axis, dim in sides:
        count = lax.axis_size(axis)
        forward = [(i, i + 1) for i in range(count - 1)]
        backward = [(target, source) for source, target in forward]
        low = lax.ppermute(
            lax.slice_in_dim(block, block.shape[dim] - width, None, axis=dim), axis, forward
        )
        high = lax.ppermute(lax.slice_in_dim(block, 0, width, axis=dim), axis, backward)
        block = jnp.concatenate([low, block, high], axis=dim)
    return block


def smooth_valid(padded):
    planes = padded.shape[0] - 8
    along_z = gauss_taps[0] * padded[0:planes].astype(jnp.float32)
    for offset in range(1, 9):
        along_z = along_z + gauss_taps[offset] * padded[offset : offset + planes].astype(
            jnp.float32
        )
    width_x = padded.shape[1] - 8
    along_x = gauss_taps[0] * along_z[:, 0:width_x]
    for offset in range(1, 9):
        along_x = along_x + gauss_taps[offset] * along_z[:, offset : offset + width_x]
    width_y = padded.shape[2] - 8
    along_y = gauss_taps[0] * along_x[:, :, 0:width_y]
    for offset in range(1, 9):
        along_y = along_y + gauss_taps[offset] * along_x[:, :, offset : offset + width_y]
    return along_y


def pair_smooth(field, axis):
    length = field.shape[axis] - 2
    lower = lax.slice_in_dim(field, 0, length, axis=axis)
    middle = lax.slice_in_dim(field, 1, length + 1, axis=axis)
    upper = lax.slice_in_dim(field, 2, length + 2, axis=axis)
    return 0.25 * lower + 0.5 * middle + 0.25 * upper


def pair_slope(field, axis):
    length = field.shape[axis] - 2
    lower = lax.slice_in_dim(field, 0, length, axis=axis)
    upper = lax.slice_in_dim(field, 2, length + 2, axis=axis)
    return 0.5 * (upper - lower)


def features(indicator, layers):
    blur_z = pair_smooth(indicator, 0)
    slope_z = pair_slope(indicator, 0)
    grad_z = pair_smooth(pair_smooth(slope_z, 1), 2)
    grad_x = pair_smooth(pair_slope(blur_z, 1), 2)
    grad_y = pair_slope(pair_smooth(blur_z, 1), 2)
    inner = indicator[1:-1, 1:-1, 1:-1]
    cells_x = inner.shape[1] // 4
    cells_y = inner.shape[2] // 4

    def blocks(field):
        return field.reshape(layers, 4, cells_x, 4, cells_y, 4)

    inner_blocks = blocks(inner)
    fraction = jnp.mean(inner_blocks, axis=(1, 3, 5))
    aperture_z = jnp.mean(inner_blocks[:, 0], axis=(2, 4))
    aperture_x = jnp.mean(inner_blocks[:, :, :, 0], axis=(1, 4))
    aperture_y = jnp.mean(inner_blocks[..., 0], axis=(1, 3))
    mean_z = jnp.mean(blocks(grad_z), axis=(1, 3, 5))
    mean_x = jnp.mean(blocks(grad_x), axis=(1, 3, 5))
    mean_y = jnp.mean(blocks(grad_y), axis=(1, 3, 5))
    length = jnp.sqrt(mean_z * mean_z + mean_x * mean_x + mean_y * mean_y + normal_floor)
    return jnp.stack(
        [
            fraction,
            aperture_z,
            aperture_x,
            aperture_y,
            -mean_z / length,
            -mean_x / length,
            -mean_y / length,
        ]
    )


def exchange_kernel(count_x, count_y, src_ref, dst_ref, own_sem, send_sem, recv_sem):
    count = count_x * count_y
    me = lax.axis_index("gx") * count_y + lax.axis_index("gy")
    barrier = pltpu.get_barrier_semaphore()

    def place(step):
        other = lax.rem(me + step, count)
        return other, (other // count_y, lax.rem(other, count_y))

    def greet(step, carry):
        pl.semaphore_signal(
            barrier, inc=1, device_id=place(step)[1], device_id_type=pl.DeviceIdType.MESH
        )
        return carry

    lax.fori_loop(1, count, greet, 0)
    pl.semaphore_wait(barrier, count - 1)

    def send(step, carry):
        other, device = place(step)
        pltpu.make_async_remote_copy(
            src_ref=src_ref.at[other],
            dst_ref=dst_ref.at[me],
            send_sem=send_sem,
            recv_sem=recv_sem,
            device_id=device,
            device_id_type=pl.DeviceIdType.MESH,
        ).start()
        return carry

    lax.fori_loop(1, count, send, 0)
    own = pltpu.make_async_copy(src_ref.at[me], dst_ref.at[me], own_sem)
    own.start()
    own.wait()
    most = pl.ds(0, count - 1)
    every = pltpu.make_async_remote_copy(
        src_ref=src_ref.at[most],
        dst_ref=dst_ref.at[most],
        send_sem=send_sem,
        recv_sem=recv_sem,
        device_id=place(1)[1],
        device_id_type=pl.DeviceIdType.MESH,
    )
    every.wait_send()
    every.wait_recv()


def exchange(outgoing, count_x, count_y):
    return pl.pallas_call(
        functools.partial(exchange_kernel, count_x, count_y),
        out_shape=jax.ShapeDtypeStruct(outgoing.shape, outgoing.dtype),
        in_specs=[pl.BlockSpec(memory_space=pltpu.VMEM)],
        out_specs=pl.BlockSpec(memory_space=pltpu.VMEM),
        scratch_shapes=[pltpu.SemaphoreType.DMA] * 3,
        compiler_params=pltpu.CompilerParams(
            collective_id=0, has_side_effects=True, vmem_limit_bytes=16 * 2**20
        ),
    )(outgoing)


def body(volume, owner, flags):
    tile_x = volume.shape[1]
    tile_y = volume.shape[2]
    layers = (volume.shape[0] - 10) // 4
    count_x = lax.axis_size("gx")
    count_y = lax.axis_size("gy")
    padded = with_halo(volume, (("gx", 1), ("gy", 2)), 5)
    smooth = smooth_valid(padded)
    place_x = lax.axis_index("gx") * tile_x - 1 + jnp.arange(tile_x + 2, dtype=jnp.int32)
    place_y = lax.axis_index("gy") * tile_y - 1 + jnp.arange(tile_y + 2, dtype=jnp.int32)
    inside_x = (place_x >= 0) & (place_x < count_x * tile_x)
    inside_y = (place_y >= 0) & (place_y < count_y * tile_y)
    inside = inside_x[None, :, None] & inside_y[None, None, :]
    indicator = jnp.where(inside, jax.nn.sigmoid(sharpness * smooth), 0.0)
    geometry = features(indicator, layers)
    cells_y = geometry.shape[3]
    row_count = layers * geometry.shape[2]
    rows_out = jnp.transpose(geometry.reshape(7, row_count, cells_y), (1, 0, 2))
    owners_local = owner.reshape(row_count)
    flags_local = flags.reshape(row_count)
    device_count = count_x * count_y
    capacity = max(2, 2 * row_count // device_count)
    targets = jnp.arange(device_count, dtype=jnp.int32)
    chosen = ((owners_local[:, None] == targets[None, :]) & (flags_local[:, None] == 1)).astype(
        jnp.int32
    )
    before = jnp.cumsum(chosen, axis=0) - chosen
    slots = jnp.sum(before * chosen, axis=1)
    dump = device_count * capacity
    target = jnp.where(flags_local == 1, owners_local * capacity + slots, dump)
    buffer = jnp.zeros((dump + 1, 7, cells_y), jnp.float32).at[target].set(rows_out)
    outgoing = buffer[:-1].reshape(device_count, capacity, 7, cells_y)
    outgoing = outgoing.reshape(device_count, capacity * 7, cells_y)
    arrived = exchange(outgoing, count_x, count_y)
    received = arrived.reshape(1, device_count * capacity, 7, cells_y)
    return (geometry, received)


def solution(mesh):
    in_specs = (P(None, "gx", "gy"), P("gx", "gy", None, None), P("gx", "gy", None))
    out_specs = (P(None, None, "gx", "gy"), P(("gx", "gy"), None, None, None))
    return jax.shard_map(body, mesh=mesh, in_specs=in_specs, out_specs=out_specs, check_vma=False)
```

```python
import functools
import math

import jax
import jax.numpy as jnp
import ml_dtypes
import numpy as np
from jax import lax
from jax.experimental import pallas as pl
from jax.experimental.pallas import tpu as pltpu
from jax.sharding import PartitionSpec as P

MESH = pl.DeviceIdType.MESH

raw_taps = [math.exp(-((offset - 4) ** 2) / 8.0) for offset in range(9)]
gauss_taps = np.array([value / sum(raw_taps) for value in raw_taps])
sharpness = 20.0
normal_floor = 0.01

PLANES_IN = 26
TILE_X = 32
TILE_Y = 512
REACH = 5
GROUPS = 3
GROUP_PLANES = 6
WIDE_X = TILE_X + 2
GROUP_ROWS = 208
GROUP_IN = GROUP_PLANES + 8
SIDE_ROWS = 144
WINDOW = 96
WINDOW_AT = [(REACH * GROUP_PLANES * g) // 16 * 16 for g in range(GROUPS)]
ROWS = 32
CHANNELS = 7
LEVELS = 32766.0


def halves(matrix):
    high = matrix.astype(np.float32).astype(ml_dtypes.bfloat16)
    low = (matrix - high.astype(np.float64)).astype(np.float32).astype(ml_dtypes.bfloat16)
    return np.stack([high, low])


def pack_matrix():
    matrix = np.zeros((2 * SIDE_ROWS, PLANES_IN * TILE_X))
    for z in range(PLANES_IN):
        for i in range(REACH):
            matrix[z * REACH + i, z * TILE_X + i] = 1
            matrix[SIDE_ROWS + z * REACH + i, z * TILE_X + TILE_X - REACH + i] = 1
    return matrix.astype(ml_dtypes.bfloat16)


def tap(distance):
    return gauss_taps[distance + 4] if -4 <= distance <= 4 else 0.0


def own_matrix():
    matrix = np.zeros((GROUP_ROWS, GROUP_IN * TILE_X))
    for plane in range(GROUP_PLANES):
        for x in range(WIDE_X):
            for z in range(9):
                for source in range(TILE_X):
                    matrix[plane * WIDE_X + x, (plane + z) * TILE_X + source] = (
                        gauss_taps[z] * tap(source - (x - 1))
                    )
    return halves(matrix)


def side_matrices():
    found = []
    for g in range(GROUPS):
        matrix = np.zeros((GROUP_ROWS, 2 * WINDOW))
        for plane in range(GROUP_PLANES):
            for x in range(WIDE_X):
                for z in range(9):
                    for i in range(REACH):
                        row = (g * GROUP_PLANES + plane + z) * REACH + i - WINDOW_AT[g]
                        out = plane * WIDE_X + x
                        matrix[out, row] = gauss_taps[z] * tap(i - REACH - (x - 1))
                        matrix[out, WINDOW + row] = gauss_taps[z] * tap(TILE_X + i - (x - 1))
        found.append(halves(matrix))
    return np.stack(found)


def along_y_matrices():
    scale = -sharpness / math.log(2.0)
    main = np.zeros((512, 256))
    for out in range(256):
        for distance in range(-4, 5):
            main[128 + out + distance, out] = scale * tap(distance)
    edge = np.zeros((512, 128))
    for distance in range(-4, 5):
        edge[127 + distance, 0] = scale * tap(distance)
        edge[384 + distance, 1] = scale * tap(distance)
    return halves(main), halves(edge)


MEAN = np.array([0, 1, 1, 1, 1, 0]) / 4
FIRST = np.array([0, 1, 0, 0, 0, 0]) / 1
SOFT = np.array([1, 3, 4, 4, 3, 1]) / 16
SLOPE = np.array([-1, -1, 0, 0, 1, 1]) / 8


def cell_matrix():
    pairs = [(MEAN, MEAN), (FIRST, MEAN), (MEAN, FIRST), (SLOPE, SOFT), (SOFT, SLOPE), (SOFT, SOFT)]
    matrix = np.zeros((GROUPS, len(pairs) * ROWS, GROUP_ROWS))
    for at, (along_z, along_x) in enumerate(pairs):
        for layer in range(4):
            for cell in range(8):
                for z in range(6):
                    for x in range(6):
                        plane = 4 * layer + z
                        place = plane % GROUP_PLANES * WIDE_X + 4 * cell + x
                        matrix[plane // GROUP_PLANES, at * ROWS + layer * 8 + cell, place] += (
                            along_z[z] * along_x[x]
                        )
    return matrix.astype(ml_dtypes.bfloat16)


def cell_y_matrix():
    matrix = np.zeros((2, TILE_Y + 128, 256))
    for at, weights in enumerate((MEAN, FIRST, SOFT, SLOPE)):
        for cell in range(128):
            for y in range(6):
                place = 4 * cell + y - 1
                row = TILE_Y if place < 0 else TILE_Y + 1 if place >= TILE_Y else place
                matrix[at // 2, row, at % 2 * 128 + cell] = weights[y]
    return matrix.astype(ml_dtypes.bfloat16)


def side_marks():
    marks = np.zeros((8, GROUP_ROWS), np.float32)
    for plane in range(GROUP_PLANES):
        marks[0, plane * WIDE_X] = 1
        marks[1, plane * WIDE_X + WIDE_X - 1] = 1
    return marks


def split(value):
    high = value.astype(jnp.bfloat16)
    return high, (value - high.astype(jnp.float32)).astype(jnp.bfloat16)


def dot(left, right):
    return jnp.dot(left, right, preferred_element_type=jnp.float32)


def routing(owner, flags):
    wide = (ROWS, ROWS)
    row = lax.broadcasted_iota(jnp.int32, wide, 0)
    column = lax.broadcasted_iota(jnp.int32, wide, 1)
    owner_across = jnp.broadcast_to(owner.astype(jnp.float32), wide)
    flag_across = jnp.broadcast_to(flags.astype(jnp.float32), wide)
    same = row == column
    owner_down = jnp.sum(jnp.where(same, owner_across, 0.0), axis=1, keepdims=True)
    flag_down = jnp.sum(jnp.where(same, flag_across, 0.0), axis=1, keepdims=True)
    earlier = (column < row) & (owner_down == owner_across)
    slot = jnp.sum(jnp.where(earlier, flag_across, 0.0), axis=1, keepdims=True)
    code = jnp.where(flag_down > 0.5, owner_down * 2.0 + slot, -8.0)
    place = lax.broadcasted_iota(jnp.int32, (ROWS, 256), 1)
    mine = (place & (ROWS - 1)) == lax.broadcasted_iota(jnp.int32, (ROWS, 256), 0)
    spread = jnp.sum(jnp.where(mine, code, 0.0), axis=0, keepdims=True)
    part = ((lax.broadcasted_iota(jnp.int32, (1, 256), 1) >> 5) & 3).astype(jnp.float32)
    return spread * 4.0 + part


def kernel(
    count_x, count_y,
    volume, owner, flags, marks, pack_w, own_w, side_w, main_w, edge_w, cell_w, cell_y_w,
    geometry, arrived,
    tile, packed, sides, smooth, chosen, leaving,
    pack_v, own_v, side_v, main_v, edge_v, cell_v, cell_y_v,
    load_sem, send_sem, recv_sem, far_sem, out_send, out_recv,
):
    p = lax.axis_index("gx")
    q = lax.axis_index("gy")
    count = count_x * count_y
    me = p * count_y + q

    def at(dx, dy):
        return (lax.rem(p + dx + count_x, count_x), lax.rem(q + dy + count_y, count_y))

    around = [(dx, dy) for dx in (-1, 0, 1) for dy in (-1, 0, 1) if (dx, dy) != (0, 0)]
    barrier = pltpu.get_barrier_semaphore()
    loads = [
        pltpu.make_async_copy(source, target, load_sem.at[i])
        for i, (source, target) in enumerate(
            [
                (volume, tile.at[:, :, pl.ds(128, TILE_Y)]),
                (pack_w, pack_v),
                (own_w, own_v),
                (side_w, side_v),
                (main_w, main_v),
                (edge_w, edge_v),
                (cell_w, cell_v),
                (cell_y_w, cell_y_v),
            ]
        )
    ]
    for load in loads:
        load.start()
    for dx, dy in around:
        pl.semaphore_signal(barrier, inc=1, device_id=at(dx, dy), device_id_type=MESH)

    loads[0].wait()
    loads[1].wait()
    own = tile[:, :, 128:640].reshape(PLANES_IN * TILE_X, TILE_Y)
    packed[...] = dot(pack_v[...], own).astype(jnp.bfloat16)

    pl.semaphore_wait(barrier, len(around))
    for dx, dy in around:
        pl.semaphore_signal(far_sem.at[0], inc=1, device_id=at(dx, dy), device_id_type=MESH)
    sends = []
    for i, (dx, dy) in enumerate(around):
        there = pl.ds(640, 128) if dy < 0 else pl.ds(0, 128)
        if dx == 0:
            source = tile.at[:, :, pl.ds(128 if dy < 0 else 512, 128)]
            target = tile.at[:, :, there]
        else:
            rows = pl.ds(0 if dx < 0 else SIDE_ROWS, SIDE_ROWS)
            rows_there = pl.ds(SIDE_ROWS if dx < 0 else 0, SIDE_ROWS)
            if dy == 0:
                source = packed.at[rows, :]
                target = sides.at[rows_there, pl.ds(128, TILE_Y)]
            else:
                source = packed.at[rows, pl.ds(0 if dy < 0 else TILE_Y - 128, 128)]
                target = sides.at[rows_there, there]
        sends.append(
            pltpu.make_async_remote_copy(
                src_ref=source,
                dst_ref=target,
                send_sem=send_sem.at[i],
                recv_sem=recv_sem.at[i],
                device_id=at(dx, dy),
                device_id_type=MESH,
            )
        )
    for send in sends:
        send.start()

    loads[2].wait()
    for g in range(GROUPS):
        block = tile[g * GROUP_PLANES : g * GROUP_PLANES + GROUP_IN, :, 128:640].reshape(
            GROUP_IN * TILE_X, TILE_Y
        )
        smooth[g] = dot(own_v[0], block) + dot(own_v[1], block)

    codes = routing(owner[...], flags[...])
    number = lax.broadcasted_iota(jnp.int32, (count * 8, 256), 0).astype(jnp.float32)
    chosen[...] = jnp.where(number == codes, 1.0, 0.0).astype(jnp.bfloat16)

    pl.semaphore_wait(far_sem.at[0], len(around))
    for dx, dy in around:
        pl.semaphore_signal(
            far_sem.at[1], inc=1, device_id=at(2 * dx, 2 * dy), device_id_type=MESH
        )
    for load in loads[3:]:
        load.wait()
    for send in sends:
        send.wait()

    @pl.when(p == 0)
    def _():
        sides[0:SIDE_ROWS, :] = jnp.zeros((SIDE_ROWS, 768), jnp.bfloat16)

    @pl.when(p == count_x - 1)
    def _():
        sides[SIDE_ROWS : 2 * SIDE_ROWS, :] = jnp.zeros((SIDE_ROWS, 768), jnp.bfloat16)

    @pl.when(q == 0)
    def _():
        sides[:, 0:128] = jnp.zeros((2 * SIDE_ROWS, 128), jnp.bfloat16)
        tile[:, :, 0:128] = jnp.zeros((PLANES_IN, TILE_X, 128), jnp.bfloat16)

    @pl.when(q == count_y - 1)
    def _():
        sides[:, 640:768] = jnp.zeros((2 * SIDE_ROWS, 128), jnp.bfloat16)
        tile[:, :, 640:768] = jnp.zeros((PLANES_IN, TILE_X, 128), jnp.bfloat16)

    pl.semaphore_wait(far_sem.at[1], len(around))
    for dx in (-4, 4):
        pl.semaphore_signal(far_sem.at[2], inc=1, device_id=at(dx, 0), device_id_type=MESH)

    low_out = jnp.where(p == 0, 1.0, 0.0)
    high_out = jnp.where(p == count_x - 1, 1.0, 0.0)
    keep = (1.0 - low_out * marks[0:1, :] - high_out * marks[1:2, :]).astype(jnp.bfloat16)
    lane = lax.broadcasted_iota(jnp.int32, (1, 128), 1)
    left_out = jnp.where(q == 0, 0, -1)
    right_out = jnp.where(q == count_y - 1, 1, -1)
    edge_keep = jnp.where((lane == left_out) | (lane == right_out), 0.0, 1.0)

    def indicator(power):
        below = 1.0 + jnp.exp2(jnp.minimum(power, 126.0))
        guess = pl.reciprocal(below, approx=True)
        return guess * (2.0 - below * guess)

    cells = jnp.zeros((6 * ROWS, TILE_Y + 128), jnp.float32)
    for g in range(GROUPS):
        planes = slice(g * GROUP_PLANES, g * GROUP_PLANES + GROUP_IN)
        ends = jnp.concatenate([tile[planes, :, 0:128], tile[planes, :, 640:768]], axis=2).reshape(
            GROUP_IN * TILE_X, 256
        )
        first = WINDOW_AT[g]
        window = jnp.concatenate(
            [
                sides[first : first + WINDOW, :],
                sides[SIDE_ROWS + first : SIDE_ROWS + first + WINDOW, :],
            ],
            axis=0,
        )
        middle = (
            dot(side_v[g, 0], window[:, 128:640])
            + dot(side_v[g, 1], window[:, 128:640])
            + smooth[g]
        )
        beside = jnp.concatenate([window[:, 0:128], window[:, 640:768]], axis=1)
        outer = (
            dot(own_v[0], ends)
            + dot(own_v[1], ends)
            + dot(side_v[g, 0], beside)
            + dot(side_v[g, 1], beside)
        )
        high, low = split(
            jnp.concatenate([outer[:, 0:128], middle, outer[:, 128:256]], axis=1)
        )
        values = []
        for c in range(2):
            lanes = slice(256 * c, 256 * c + 512)
            values.append(
                indicator(
                    dot(high[:, lanes], main_v[0])
                    + dot(low[:, lanes], main_v[0])
                    + dot(high[:, lanes], main_v[1])
                )
            )
        high_edge = jnp.concatenate([high[:, 0:256], high[:, 512:768]], axis=1)
        low_edge = jnp.concatenate([low[:, 0:256], low[:, 512:768]], axis=1)
        values.append(
            edge_keep
            * indicator(
                dot(high_edge, edge_v[0]) + dot(low_edge, edge_v[0]) + dot(high_edge, edge_v[1])
            )
        )
        high, low = split(jnp.concatenate(values, axis=1))
        weights = cell_v[g] * keep
        cells = cells + dot(weights, high) + dot(weights, low)

    high, low = split(cells)
    plain = dot(high[0:96], cell_y_v[0]) + dot(low[0:96], cell_y_v[0])
    slopes = dot(high[96:192], cell_y_v[1]) + dot(low[96:192], cell_y_v[1])
    mean_z, mean_x, mean_y = slopes[0:32, 0:128], slopes[32:64, 0:128], slopes[64:96, 128:256]
    shrink = -lax.rsqrt(mean_z * mean_z + mean_x * mean_x + mean_y * mean_y + normal_floor)
    found = [
        plain[0:32, 0:128],
        plain[32:64, 0:128],
        plain[64:96, 0:128],
        plain[0:32, 128:256],
        mean_z * shrink,
        mean_x * shrink,
        mean_y * shrink,
    ]
    for channel in range(CHANNELS):
        geometry[channel] = found[channel]

    most = functools.reduce(jnp.maximum, [jnp.abs(value) for value in found])
    most = jnp.maximum(jnp.max(most, axis=1, keepdims=True), 1e-37)
    grade = jnp.ceil(8.0 * jnp.log2(most) + 0.02)
    stretch = jnp.exp2(grade * -0.125)
    whole = [jnp.floor(value * stretch * LEVELS + 0.5) for value in found]
    whole.append(jnp.broadcast_to(grade, (ROWS, 128)))
    coded = jnp.concatenate(
        [jnp.concatenate(whole[0:4], axis=0), jnp.concatenate(whole[4:8], axis=0)], axis=1
    )
    upper = jnp.floor(coded * (1.0 / 256.0) + 0.5) * 256.0
    stacked = jnp.concatenate([upper, coded - upper], axis=0).astype(jnp.bfloat16)
    placed = dot(chosen[...], stacked).astype(jnp.int32)
    joined = (placed[:, 128:256] << 16) | (placed[:, 0:128] & 0xFFFF)
    leaving[...] = joined.reshape(count, 8, 128)

    pl.semaphore_wait(far_sem.at[2], 2)

    def send_out(step, carry):
        other = lax.rem(me + step, count)
        pltpu.make_async_remote_copy(
            src_ref=leaving.at[other],
            dst_ref=arrived.at[me],
            send_sem=out_send,
            recv_sem=out_recv,
            device_id=(other // count_y, lax.rem(other, count_y)),
            device_id_type=MESH,
        ).start()
        return carry

    lax.fori_loop(1, count, send_out, 0)
    arrived[me] = leaving[me]
    others = pl.ds(0, count - 1)
    every = pltpu.make_async_remote_copy(
        src_ref=leaving.at[others],
        dst_ref=arrived.at[others],
        send_sem=out_send,
        recv_sem=out_recv,
        device_id=at(1, 0),
        device_id_type=MESH,
    )
    every.wait_send()
    every.wait_recv()


def decode_kernel(coded, geometry_in, received, geometry):
    geometry[...] = geometry_in[...]
    rows = received.shape[1]

    def pair(part):
        both = coded[pl.ds(part, rows, stride=4), :]
        return (both << 16) >> 16, both >> 16

    fourth, grade = pair(3)
    scale = jnp.exp2(grade.astype(jnp.float32) * 0.125) * (1.0 / LEVELS)
    received[3] = fourth.astype(jnp.float32) * scale
    for part in range(3):
        low, high = pair(part)
        received[part] = low.astype(jnp.float32) * scale
        received[part + 4] = high.astype(jnp.float32) * scale


def body(count_x, count_y, volume, owner, flags):
    count = count_x * count_y
    main_w, edge_w = along_y_matrices()
    weights = [
        pack_matrix(), own_matrix(), side_matrices(), main_w, edge_w, cell_matrix(), cell_y_matrix(),
    ]
    in_vmem = pl.BlockSpec(memory_space=pltpu.VMEM)
    anywhere = pl.BlockSpec(memory_space=pl.ANY)
    geometry, arrived = pl.pallas_call(
        functools.partial(kernel, count_x, count_y),
        out_shape=(
            jax.ShapeDtypeStruct((CHANNELS, ROWS, 128), jnp.float32),
            jax.ShapeDtypeStruct((count, 8, 128), jnp.int32),
        ),
        in_specs=[anywhere, in_vmem, in_vmem, in_vmem] + [anywhere] * len(weights),
        out_specs=(in_vmem, in_vmem),
        scratch_shapes=[
            pltpu.VMEM((PLANES_IN, TILE_X, 768), jnp.bfloat16),
            pltpu.VMEM((2 * SIDE_ROWS, TILE_Y), jnp.bfloat16),
            pltpu.VMEM((2 * SIDE_ROWS, 768), jnp.bfloat16),
            pltpu.VMEM((GROUPS, GROUP_ROWS, TILE_Y), jnp.float32),
            pltpu.VMEM((count * 8, 256), jnp.bfloat16),
            pltpu.VMEM((count, 8, 128), jnp.int32),
        ]
        + [pltpu.VMEM(weight.shape, jnp.bfloat16) for weight in weights]
        + [
            pltpu.SemaphoreType.DMA((1 + len(weights),)),
            pltpu.SemaphoreType.DMA((8,)),
            pltpu.SemaphoreType.DMA((8,)),
            pltpu.SemaphoreType.REGULAR((3,)),
            pltpu.SemaphoreType.DMA,
            pltpu.SemaphoreType.DMA,
        ],
        compiler_params=pltpu.CompilerParams(
            collective_id=0, has_side_effects=True, vmem_limit_bytes=62 * 2**20
        ),
    )(volume, owner.reshape(1, ROWS), flags.reshape(1, ROWS), side_marks(), *weights)
    received, geometry = pl.pallas_call(
        decode_kernel,
        out_shape=(
            jax.ShapeDtypeStruct((CHANNELS, count * 2, 128), jnp.float32),
            jax.ShapeDtypeStruct(geometry.shape, jnp.float32),
        ),
        in_specs=[in_vmem, in_vmem],
        out_specs=(in_vmem, in_vmem),
        compiler_params=pltpu.CompilerParams(vmem_limit_bytes=16 * 2**20),
    )(arrived.reshape(count * 8, 128), geometry)
    received = jnp.transpose(received, (1, 0, 2))[None]
    return (geometry.reshape(CHANNELS, 4, 8, 128), received)


def solution(mesh):
    in_specs = (P(None, "gx", "gy"), P("gx", "gy", None, None), P("gx", "gy", None))
    out_specs = (P(None, None, "gx", "gy"), P(("gx", "gy"), None, None, None))
    return jax.shard_map(
        functools.partial(body, mesh.shape["gx"], mesh.shape["gy"]),
        mesh=mesh,
        in_specs=in_specs,
        out_specs=out_specs,
        check_vma=False,
    )
```

```python
import functools
import math

import jax
import jax.numpy as jnp
import ml_dtypes
import numpy as np
from jax import lax
from jax.experimental import pallas as pl
from jax.experimental.pallas import tpu as pltpu
from jax.sharding import PartitionSpec as P

MESH = pl.DeviceIdType.MESH

raw_taps = [math.exp(-((offset - 4) ** 2) / 8.0) for offset in range(9)]
gauss_taps = np.array([value / sum(raw_taps) for value in raw_taps])
sharpness = 20.0
normal_floor = 0.01

PLANES_IN = 26
TILE_X = 32
TILE_Y = 512
OWN = PLANES_IN * TILE_X
REACH = 5
WIDE_X = TILE_X + 2
GROUPS = 3
GROUP_PLANES = 6
GROUP_IN = GROUP_PLANES + 8
INNER_X = 24
OUTER_X = 10
INNER = GROUP_PLANES * INNER_X
OUTER = 64
GROUP_ROWS = INNER + OUTER
SIDE_ROWS = 144
WINDOW = 96
WINDOW_AT = [(REACH * GROUP_PLANES * g) // 16 * 16 for g in range(GROUPS)]
WIDE_Y = TILE_Y + 128
ROWS = 32
CHANNELS = 7
LEVELS = 32766.0


def outer_place(x):
    if x < REACH:
        return x
    return x - INNER_X if x >= REACH + INNER_X else None


def row_of(plane, x):
    outer = outer_place(x)
    if outer is None:
        return plane * INNER_X + x - REACH
    return INNER + plane * OUTER_X + outer


def halves(matrix):
    high = matrix.astype(np.float32).astype(ml_dtypes.bfloat16)
    low = (matrix - high.astype(np.float64)).astype(np.float32).astype(ml_dtypes.bfloat16)
    return np.stack([high, low])


def pack_matrix():
    matrix = np.zeros((2 * SIDE_ROWS, OWN))
    for z in range(PLANES_IN):
        for i in range(REACH):
            matrix[z * REACH + i, z * TILE_X + i] = 1
            matrix[SIDE_ROWS + z * REACH + i, z * TILE_X + TILE_X - REACH + i] = 1
    return matrix.astype(ml_dtypes.bfloat16)


def column_matrices():
    take = np.zeros((32, 256))
    put = np.zeros((32, 128))
    for i in range(REACH):
        take[i, i] = 1
        take[16 + i, 256 - REACH + i] = 1
        put[i, 128 - REACH + i] = 1
        put[16 + i, i] = 1
    return take.astype(ml_dtypes.bfloat16), put.astype(ml_dtypes.bfloat16)


def tap(distance):
    return gauss_taps[distance + 4] if -4 <= distance <= 4 else 0.0


def own_matrix():
    matrix = np.zeros((GROUP_ROWS, GROUP_IN * TILE_X))
    for plane in range(GROUP_PLANES):
        for x in range(WIDE_X):
            for z in range(9):
                for source in range(TILE_X):
                    matrix[row_of(plane, x), (plane + z) * TILE_X + source] = (
                        gauss_taps[z] * tap(source - (x - 1))
                    )
    return halves(matrix)


def side_matrices():
    found = []
    for g in range(GROUPS):
        matrix = np.zeros((OUTER, 2 * WINDOW))
        for plane in range(GROUP_PLANES):
            for x in range(WIDE_X):
                outer = outer_place(x)
                if outer is None:
                    continue
                for z in range(9):
                    for i in range(REACH):
                        row = (g * GROUP_PLANES + plane + z) * REACH + i - WINDOW_AT[g]
                        out = plane * OUTER_X + outer
                        matrix[out, row] = gauss_taps[z] * tap(i - REACH - (x - 1))
                        matrix[out, WINDOW + row] = gauss_taps[z] * tap(TILE_X + i - (x - 1))
        found.append(halves(matrix))
    return np.stack(found)


def along_y_matrices():
    scale = -sharpness / math.log(2.0)
    main = np.zeros((512, 256))
    for out in range(256):
        for distance in range(-4, 5):
            main[128 + out + distance, out] = scale * tap(distance)
    edge = np.zeros((512, 128))
    for distance in range(-4, 5):
        edge[127 + distance, 0] = scale * tap(distance)
        edge[384 + distance, 1] = scale * tap(distance)
    return halves(main), halves(edge)


MEAN = np.array([0, 1, 1, 1, 1, 0]) / 4
FIRST = np.array([0, 1, 0, 0, 0, 0]) / 1
SOFT = np.array([1, 3, 4, 4, 3, 1]) / 16
SLOPE = np.array([-1, -1, 0, 0, 1, 1]) / 8


def cell_matrices():
    pairs = [(MEAN, MEAN), (FIRST, MEAN), (MEAN, FIRST), (SLOPE, SOFT), (SOFT, SLOPE), (SOFT, SOFT)]
    inner = np.zeros((len(pairs) * ROWS, GROUPS * INNER))
    outer = np.zeros((len(pairs) * ROWS, GROUPS * OUTER))
    for at, (along_z, along_x) in enumerate(pairs):
        for layer in range(4):
            for cell in range(8):
                for z in range(6):
                    for x in range(6):
                        group, plane = divmod(4 * layer + z, GROUP_PLANES)
                        row = row_of(plane, 4 * cell + x)
                        out = at * ROWS + layer * 8 + cell
                        weight = along_z[z] * along_x[x]
                        if row < INNER:
                            inner[out, group * INNER + row] += weight
                        else:
                            outer[out, group * OUTER + row - INNER] += weight
    return inner.astype(ml_dtypes.bfloat16), outer.astype(ml_dtypes.bfloat16)


def cell_y_matrix():
    matrix = np.zeros((2, TILE_Y + 128, 256))
    for at, weights in enumerate((MEAN, FIRST, SOFT, SLOPE)):
        for cell in range(128):
            for y in range(6):
                place = 4 * cell + y - 1
                row = TILE_Y if place < 0 else TILE_Y + 1 if place >= TILE_Y else place
                matrix[at // 2, row, at % 2 * 128 + cell] = weights[y]
    return matrix.astype(ml_dtypes.bfloat16)


def side_marks():
    marks = np.zeros((8, GROUPS * OUTER), np.float32)
    for group in range(GROUPS):
        for plane in range(GROUP_PLANES):
            marks[0, group * OUTER + plane * OUTER_X] = 1
            marks[1, group * OUTER + plane * OUTER_X + OUTER_X - 1] = 1
    return marks


def split(value):
    high = value.astype(jnp.bfloat16)
    return high, (value - high.astype(jnp.float32)).astype(jnp.bfloat16)


def dot(left, right):
    return jnp.dot(left, right, preferred_element_type=jnp.float32)


def routing(owner, flags):
    wide = (ROWS, ROWS)
    row = lax.broadcasted_iota(jnp.int32, wide, 0)
    column = lax.broadcasted_iota(jnp.int32, wide, 1)
    owner_across = jnp.broadcast_to(owner.astype(jnp.float32), wide)
    flag_across = jnp.broadcast_to(flags.astype(jnp.float32), wide)
    same = row == column
    owner_down = jnp.sum(jnp.where(same, owner_across, 0.0), axis=1, keepdims=True)
    flag_down = jnp.sum(jnp.where(same, flag_across, 0.0), axis=1, keepdims=True)
    earlier = (column < row) & (owner_down == owner_across)
    slot = jnp.sum(jnp.where(earlier, flag_across, 0.0), axis=1, keepdims=True)
    code = jnp.where(flag_down > 0.5, owner_down * 2.0 + slot, -8.0)
    place = lax.broadcasted_iota(jnp.int32, (ROWS, 256), 1)
    mine = (place & (ROWS - 1)) == lax.broadcasted_iota(jnp.int32, (ROWS, 256), 0)
    spread = jnp.sum(jnp.where(mine, code, 0.0), axis=0, keepdims=True)
    part = ((lax.broadcasted_iota(jnp.int32, (1, 256), 1) >> 5) & 3).astype(jnp.float32)
    return spread * 4.0 + part


def kernel(
    count_x, count_y,
    volume, owner, flags, marks, put_w,
    take_w, pack_w, own_w, main_w, edge_w, inner_w, side_w, outer_w, cell_y_w,
    geometry, arrived,
    tile, packed, columns, corners, sides, beside, corner_in, ends, side_ends,
    smooth, sharp, chosen, leaving,
    take_v, pack_v, own_v, main_v, edge_v, inner_v, side_v, outer_v, cell_y_v,
    load_sem, send_sem, recv_sem, far_sem, out_send, out_recv,
):
    p = lax.axis_index("gx")
    q = lax.axis_index("gy")
    count = count_x * count_y
    me = p * count_y + q

    def at(dx, dy):
        return (lax.rem(p + dx + count_x, count_x), lax.rem(q + dy + count_y, count_y))

    around = [(0, -1), (0, 1), (-1, 0), (1, 0), (-1, -1), (-1, 1), (1, -1), (1, 1)]
    barrier = pltpu.get_barrier_semaphore()
    pairs = [
        (volume, tile),
        (take_w, take_v),
        (pack_w, pack_v),
        (own_w, own_v),
        (main_w, main_v),
        (edge_w, edge_v),
        (inner_w, inner_v),
        (side_w, side_v),
        (outer_w, outer_v),
        (cell_y_w, cell_y_v),
    ]
    loads = [pltpu.make_async_copy(*pair, load_sem.at[i]) for i, pair in enumerate(pairs)]
    for load in loads:
        load.start()
    for dx, dy in around:
        pl.semaphore_signal(barrier, inc=1, device_id=at(dx, dy), device_id_type=MESH)

    def take_columns(rows):
        both = jnp.concatenate([rows[:, 0:128], rows[:, TILE_Y - 128 : TILE_Y]], axis=1)
        return lax.dot_general(
            take_v[...], both, (((1,), (1,)), ((), ())), preferred_element_type=jnp.float32
        ).astype(jnp.bfloat16)

    def put_columns(taken):
        return lax.dot_general(
            taken, put_w[...], (((0,), (0,)), ((), ())), preferred_element_type=jnp.float32
        ).astype(jnp.bfloat16)

    for load in loads[0:3]:
        load.wait()
    own = tile[...].reshape(OWN, TILE_Y)
    edge_rows = dot(pack_v[...], own).astype(jnp.bfloat16)
    packed[...] = edge_rows
    columns[:, 0:OWN] = take_columns(own)
    for side in range(2):
        corners[side, :, 0:SIDE_ROWS] = take_columns(
            edge_rows[side * SIDE_ROWS : (side + 1) * SIDE_ROWS]
        )

    pl.semaphore_wait(barrier, len(around))
    for dx, dy in around:
        pl.semaphore_signal(far_sem.at[0], inc=1, device_id=at(dx, dy), device_id_type=MESH)
    sends = []
    for i, (dx, dy) in enumerate(around):
        rows, rows_there = (0, SIDE_ROWS) if dx < 0 else (SIDE_ROWS, 0)
        lines, lines_there = (0, 16) if dy < 0 else (16, 0)
        if dx == 0:
            source = columns.at[pl.ds(lines, 16), :]
            target = beside.at[pl.ds(lines_there, 16), :]
        elif dy == 0:
            source = packed.at[pl.ds(rows, SIDE_ROWS), :]
            target = sides.at[pl.ds(rows_there, SIDE_ROWS), :]
        else:
            source = corners.at[rows // SIDE_ROWS, pl.ds(lines, 16), :]
            target = corner_in.at[rows_there // SIDE_ROWS, pl.ds(lines_there, 16), :]
        sends.append(
            pltpu.make_async_remote_copy(
                src_ref=source,
                dst_ref=target,
                send_sem=send_sem.at[i],
                recv_sem=recv_sem.at[i],
                device_id=at(dx, dy),
                device_id_type=MESH,
            )
        )
    for send in sends:
        send.start()

    loads[3].wait()
    for g in range(GROUPS):
        block = tile[g * GROUP_PLANES : g * GROUP_PLANES + GROUP_IN].reshape(
            GROUP_IN * TILE_X, TILE_Y
        )
        smooth[g, :, 128:WIDE_Y] = dot(own_v[0], block) + dot(own_v[1], block)

    codes = routing(owner[...], flags[...])
    number = lax.broadcasted_iota(jnp.int32, (count * 8, 256), 0).astype(jnp.float32)
    chosen[...] = jnp.where(number == codes, 1.0, 0.0).astype(jnp.bfloat16)

    pl.semaphore_wait(far_sem.at[0], len(around))
    for dx, dy in around:
        pl.semaphore_signal(
            far_sem.at[1], inc=1, device_id=at(2 * dx, 2 * dy), device_id_type=MESH
        )
    for load in loads[4:]:
        load.wait()
    for send in sends[0:2]:
        send.wait()

    @pl.when(q == 0)
    def _():
        beside[0:16, :] = jnp.zeros((16, beside.shape[1]), jnp.bfloat16)

    @pl.when(q == count_y - 1)
    def _():
        beside[16:32, :] = jnp.zeros((16, beside.shape[1]), jnp.bfloat16)

    lane = lax.broadcasted_iota(jnp.int32, (1, 128), 1)
    left_out = jnp.where(q == 0, 0, -1)
    right_out = jnp.where(q == count_y - 1, 1, -1)
    edge_keep = jnp.where((lane == left_out) | (lane == right_out), 0.0, 1.0)

    def sigmoid_of(power):
        below = 1.0 + jnp.exp2(jnp.minimum(power, 126.0))
        guess = pl.reciprocal(below, approx=True)
        return guess * (2.0 - below * guess)

    def indicator(blurred):
        high, low = split(blurred)

        def along_y(choose, weights):
            high_part = choose(high)
            return sigmoid_of(
                dot(high_part, weights[0])
                + dot(choose(low), weights[0])
                + dot(high_part, weights[1])
            )

        def last(part):
            return jnp.concatenate([part[:, 256:WIDE_Y], part[:, 0:128]], axis=1)

        def ends_of(part):
            return jnp.concatenate([part[:, 0:256], part[:, 512:WIDE_Y], part[:, 0:128]], axis=1)

        return split(
            jnp.concatenate(
                [
                    along_y(lambda part: part[:, 0:512], main_v),
                    along_y(last, main_v),
                    edge_keep * along_y(ends_of, edge_v),
                ],
                axis=1,
            )
        )

    ends[...] = put_columns(beside[:, 0:OWN])
    for g in range(GROUPS):
        first = g * GROUP_PLANES * TILE_X
        block = ends[first : first + GROUP_IN * TILE_X, :]
        smooth[g, :, 0:128] = dot(own_v[0], block) + dot(own_v[1], block)
        high, low = indicator(smooth[g, 0:INNER, :])
        sharp[0, g * INNER : (g + 1) * INNER, :] = high
        sharp[1, g * INNER : (g + 1) * INNER, :] = low
    cells = dot(inner_v[...], sharp[0]) + dot(inner_v[...], sharp[1])

    pl.semaphore_wait(far_sem.at[1], len(around))
    for dx in (-4, 4):
        pl.semaphore_signal(far_sem.at[2], inc=1, device_id=at(dx, 0), device_id_type=MESH)
    for send in sends[2:]:
        send.wait()

    @pl.when(p == 0)
    def _():
        sides[0:SIDE_ROWS, :] = jnp.zeros((SIDE_ROWS, TILE_Y), jnp.bfloat16)
        corner_in[0] = jnp.zeros(corner_in.shape[1:], jnp.bfloat16)

    @pl.when(p == count_x - 1)
    def _():
        sides[SIDE_ROWS : 2 * SIDE_ROWS, :] = jnp.zeros((SIDE_ROWS, TILE_Y), jnp.bfloat16)
        corner_in[1] = jnp.zeros(corner_in.shape[1:], jnp.bfloat16)

    @pl.when(q == 0)
    def _():
        corner_in[:, 0:16, :] = jnp.zeros((2, 16, corner_in.shape[2]), jnp.bfloat16)

    @pl.when(q == count_y - 1)
    def _():
        corner_in[:, 16:32, :] = jnp.zeros((2, 16, corner_in.shape[2]), jnp.bfloat16)

    for side in range(2):
        side_ends[side * SIDE_ROWS : (side + 1) * SIDE_ROWS, :] = put_columns(
            corner_in[side, :, 0:SIDE_ROWS]
        )
    blurred = []
    for g in range(GROUPS):
        low_rows = slice(WINDOW_AT[g], WINDOW_AT[g] + WINDOW)
        high_rows = slice(SIDE_ROWS + WINDOW_AT[g], SIDE_ROWS + WINDOW_AT[g] + WINDOW)
        window = jnp.concatenate(
            [
                jnp.concatenate([side_ends[low_rows, :], sides[low_rows, :]], axis=1),
                jnp.concatenate([side_ends[high_rows, :], sides[high_rows, :]], axis=1),
            ],
            axis=0,
        )
        blurred.append(
            dot(side_v[g, 0], window) + dot(side_v[g, 1], window) + smooth[g, INNER:GROUP_ROWS, :]
        )
    high, low = indicator(jnp.concatenate(blurred, axis=0))
    low_out = jnp.where(p == 0, 1.0, 0.0)
    high_out = jnp.where(p == count_x - 1, 1.0, 0.0)
    keep = (1.0 - low_out * marks[0:1, :] - high_out * marks[1:2, :]).astype(jnp.bfloat16)
    weights = outer_v[...] * keep
    cells = cells + dot(weights, high) + dot(weights, low)

    high, low = split(cells)
    plain = dot(high[0:96], cell_y_v[0]) + dot(low[0:96], cell_y_v[0])
    slopes = dot(high[96:192], cell_y_v[1]) + dot(low[96:192], cell_y_v[1])
    mean_z, mean_x, mean_y = slopes[0:32, 0:128], slopes[32:64, 0:128], slopes[64:96, 128:256]
    shrink = -lax.rsqrt(mean_z * mean_z + mean_x * mean_x + mean_y * mean_y + normal_floor)
    found = [
        plain[0:32, 0:128],
        plain[32:64, 0:128],
        plain[64:96, 0:128],
        plain[0:32, 128:256],
        mean_z * shrink,
        mean_x * shrink,
        mean_y * shrink,
    ]
    for channel in range(CHANNELS):
        geometry[channel] = found[channel]

    most = functools.reduce(jnp.maximum, [jnp.abs(value) for value in found])
    most = jnp.maximum(jnp.max(most, axis=1, keepdims=True), 1e-37)
    grade = jnp.ceil(8.0 * jnp.log2(most) + 0.02)
    stretch = jnp.exp2(grade * -0.125)
    whole = [jnp.floor(value * stretch * LEVELS + 0.5) for value in found]
    whole.append(jnp.broadcast_to(grade, (ROWS, 128)))
    coded = jnp.concatenate(
        [jnp.concatenate(whole[0:4], axis=0), jnp.concatenate(whole[4:8], axis=0)], axis=1
    )
    upper = jnp.floor(coded * (1.0 / 256.0) + 0.5) * 256.0
    stacked = jnp.concatenate([upper, coded - upper], axis=0).astype(jnp.bfloat16)
    placed = dot(chosen[...], stacked).astype(jnp.int32)
    joined = (placed[:, 128:256] << 16) | (placed[:, 0:128] & 0xFFFF)
    leaving[...] = joined.reshape(count, 8, 128)

    pl.semaphore_wait(far_sem.at[2], 2)

    def send_out(step, carry):
        other = lax.rem(me + step, count)
        pltpu.make_async_remote_copy(
            src_ref=leaving.at[other],
            dst_ref=arrived.at[me],
            send_sem=out_send,
            recv_sem=out_recv,
            device_id=(other // count_y, lax.rem(other, count_y)),
            device_id_type=MESH,
        ).start()
        return carry

    lax.fori_loop(1, count, send_out, 0)
    arrived[me] = leaving[me]
    others = pl.ds(0, count - 1)
    every = pltpu.make_async_remote_copy(
        src_ref=leaving.at[others],
        dst_ref=arrived.at[others],
        send_sem=out_send,
        recv_sem=out_recv,
        device_id=at(1, 0),
        device_id_type=MESH,
    )
    every.wait_send()
    every.wait_recv()


def decode_kernel(
    coded, geometry_in, received, geometry, coded_v, geometry_v, received_v,
    copy_sem, load_sem, store_sem,
):
    pieces = load_sem.shape[0]
    rows = received_v.shape[1] // pieces
    whole_in = pltpu.make_async_copy(geometry_in, geometry_v, copy_sem.at[0])
    whole_out = pltpu.make_async_copy(geometry_v, geometry, copy_sem.at[1])
    loads, stores = [], []
    for i in range(pieces):
        source = pl.ds(i * rows * 4, rows * 4)
        target = pl.ds(i * rows, rows)
        loads.append(
            pltpu.make_async_copy(coded.at[source, :], coded_v.at[source, :], load_sem.at[i])
        )
        stores.append(
            pltpu.make_async_copy(
                received_v.at[:, target, :], received.at[:, target, :], store_sem.at[i]
            )
        )
    for load in loads:
        load.start()
    whole_in.start()
    for i in range(pieces):
        loads[i].wait()
        target = slice(i * rows, (i + 1) * rows)

        def pair(part):
            both = coded_v[pl.ds(i * rows * 4 + part, rows, stride=4), :]
            return (both << 16) >> 16, both >> 16

        fourth, grade = pair(3)
        scale = jnp.exp2(grade.astype(jnp.float32) * 0.125) * (1.0 / LEVELS)
        received_v[3, target] = fourth.astype(jnp.float32) * scale
        for part in range(3):
            low, high = pair(part)
            received_v[part, target] = low.astype(jnp.float32) * scale
            received_v[part + 4, target] = high.astype(jnp.float32) * scale
        stores[i].start()
    whole_in.wait()
    whole_out.start()
    for store in stores:
        store.wait()
    whole_out.wait()


def body(count_x, count_y, volume, owner, flags):
    count = count_x * count_y
    main_w, edge_w = along_y_matrices()
    inner_w, outer_w = cell_matrices()
    take_w, put_w = column_matrices()
    weights = [
        take_w, pack_matrix(), own_matrix(), main_w, edge_w, inner_w, side_matrices(), outer_w, cell_y_matrix(),
    ]
    in_vmem = pl.BlockSpec(memory_space=pltpu.VMEM)
    anywhere = pl.BlockSpec(memory_space=pl.ANY)
    bf16 = jnp.bfloat16
    geometry, arrived = pl.pallas_call(
        functools.partial(kernel, count_x, count_y),
        out_shape=(
            jax.ShapeDtypeStruct((CHANNELS, ROWS, 128), jnp.float32),
            jax.ShapeDtypeStruct((count, 8, 128), jnp.int32),
        ),
        in_specs=[anywhere] + [in_vmem] * 4 + [anywhere] * len(weights),
        out_specs=(in_vmem, in_vmem),
        scratch_shapes=[
            pltpu.VMEM((PLANES_IN, TILE_X, TILE_Y), bf16),
            pltpu.VMEM((2 * SIDE_ROWS, TILE_Y), bf16),
            pltpu.VMEM((32, 896), bf16),
            pltpu.VMEM((2, 32, 256), bf16),
            pltpu.VMEM((2 * SIDE_ROWS, TILE_Y), bf16),
            pltpu.VMEM((32, 896), bf16),
            pltpu.VMEM((2, 32, 256), bf16),
            pltpu.VMEM((OWN, 128), bf16),
            pltpu.VMEM((2 * SIDE_ROWS, 128), bf16),
            pltpu.VMEM((GROUPS, GROUP_ROWS, WIDE_Y), jnp.float32),
            pltpu.VMEM((2, GROUPS * INNER, WIDE_Y), bf16),
            pltpu.VMEM((count * 8, 256), bf16),
            pltpu.VMEM((count, 8, 128), jnp.int32),
        ]
        + [pltpu.VMEM(weight.shape, bf16) for weight in weights]
        + [
            pltpu.SemaphoreType.DMA((1 + len(weights),)),
            pltpu.SemaphoreType.DMA((8,)),
            pltpu.SemaphoreType.DMA((8,)),
            pltpu.SemaphoreType.REGULAR((3,)),
            pltpu.SemaphoreType.DMA,
            pltpu.SemaphoreType.DMA,
        ],
        compiler_params=pltpu.CompilerParams(
            collective_id=0, has_side_effects=True, vmem_limit_bytes=62 * 2**20
        ),
    )(volume, owner.reshape(1, ROWS), flags.reshape(1, ROWS), side_marks(), put_w, *weights)
    pieces = 4
    received, geometry = pl.pallas_call(
        decode_kernel,
        out_shape=(
            jax.ShapeDtypeStruct((CHANNELS, count * 2, 128), jnp.float32),
            jax.ShapeDtypeStruct(geometry.shape, jnp.float32),
        ),
        in_specs=[anywhere, anywhere],
        out_specs=(anywhere, anywhere),
        scratch_shapes=[
            pltpu.VMEM((count * 8, 128), jnp.int32),
            pltpu.VMEM(geometry.shape, jnp.float32),
            pltpu.VMEM((CHANNELS, count * 2, 128), jnp.float32),
            pltpu.SemaphoreType.DMA((2,)),
            pltpu.SemaphoreType.DMA((pieces,)),
            pltpu.SemaphoreType.DMA((pieces,)),
        ],
        compiler_params=pltpu.CompilerParams(vmem_limit_bytes=62 * 2**20),
    )(arrived.reshape(count * 8, 128), geometry)
    received = jnp.transpose(received, (1, 0, 2))[None]
    return (geometry.reshape(CHANNELS, 4, 8, 128), received)


def solution(mesh):
    in_specs = (P(None, "gx", "gy"), P("gx", "gy", None, None), P("gx", "gy", None))
    out_specs = (P(None, None, "gx", "gy"), P(("gx", "gy"), None, None, None))
    return jax.shard_map(
        functools.partial(body, mesh.shape["gx"], mesh.shape["gy"]),
        mesh=mesh,
        in_specs=in_specs,
        out_specs=out_specs,
        check_vma=False,
    )
```

```python
import functools
import math

import jax
import jax.numpy as jnp
import ml_dtypes
import numpy as np
from jax import lax
from jax.experimental import pallas as pl
from jax.experimental.pallas import tpu as pltpu
from jax.sharding import PartitionSpec as P

MESH = pl.DeviceIdType.MESH

raw_taps = [math.exp(-((offset - 4) ** 2) / 8.0) for offset in range(9)]
gauss_taps = np.array([value / sum(raw_taps) for value in raw_taps])
sharpness = 20.0
normal_floor = 0.01

PLANES_IN = 26
TILE_X = 32
TILE_Y = 512
OWN = PLANES_IN * TILE_X
REACH = 5
WIDE_X = TILE_X + 2
GROUPS = 3
GROUP_PLANES = 6
GROUP_IN = GROUP_PLANES + 8
INNER_X = 24
OUTER_X = 10
INNER = GROUP_PLANES * INNER_X
OUTER = 64
GROUP_ROWS = INNER + OUTER
SIDE_ROWS = 144
WINDOW = 96
WINDOW_AT = [(REACH * GROUP_PLANES * g) // 16 * 16 for g in range(GROUPS)]
PACK_PLANES = 8
PACK_ROWS = PACK_PLANES * REACH
WIDE_Y = TILE_Y + 128
BAND = (112, 400)
ROWS = 32
CHANNELS = 7
LEVELS = 32766.0


def outer_place(x):
    if x < REACH:
        return x
    return x - INNER_X if x >= REACH + INNER_X else None


def row_of(plane, x):
    outer = outer_place(x)
    if outer is None:
        return plane * INNER_X + x - REACH
    return INNER + plane * OUTER_X + outer


def halves(matrix):
    high = matrix.astype(np.float32).astype(ml_dtypes.bfloat16)
    low = (matrix - high.astype(np.float64)).astype(np.float32).astype(ml_dtypes.bfloat16)
    return np.stack([high, low])


def pack_matrix():
    matrix = np.zeros((2 * PACK_ROWS, PACK_PLANES * TILE_X))
    for z in range(PACK_PLANES):
        for i in range(REACH):
            matrix[z * REACH + i, z * TILE_X + i] = 1
            matrix[PACK_ROWS + z * REACH + i, z * TILE_X + TILE_X - REACH + i] = 1
    return matrix.astype(ml_dtypes.bfloat16)


def column_matrices():
    take = np.zeros((32, 256))
    put = np.zeros((32, 128))
    for i in range(REACH):
        take[i, i] = 1
        take[16 + i, 256 - REACH + i] = 1
        put[i, 128 - REACH + i] = 1
        put[16 + i, i] = 1
    return take.astype(ml_dtypes.bfloat16), put.astype(ml_dtypes.bfloat16)


def tap(distance):
    return gauss_taps[distance + 4] if -4 <= distance <= 4 else 0.0


def own_matrix():
    matrix = np.zeros((GROUP_ROWS, GROUP_IN * TILE_X))
    for plane in range(GROUP_PLANES):
        for x in range(WIDE_X):
            for z in range(9):
                for source in range(TILE_X):
                    matrix[row_of(plane, x), (plane + z) * TILE_X + source] = (
                        gauss_taps[z] * tap(source - (x - 1))
                    )
    return halves(matrix)


def side_matrices():
    found = []
    for g in range(GROUPS):
        matrix = np.zeros((OUTER, 2 * WINDOW))
        for plane in range(GROUP_PLANES):
            for x in range(WIDE_X):
                outer = outer_place(x)
                if outer is None:
                    continue
                for z in range(9):
                    for i in range(REACH):
                        row = (g * GROUP_PLANES + plane + z) * REACH + i - WINDOW_AT[g]
                        out = plane * OUTER_X + outer
                        matrix[out, row] = gauss_taps[z] * tap(i - REACH - (x - 1))
                        matrix[out, WINDOW + row] = gauss_taps[z] * tap(TILE_X + i - (x - 1))
        found.append(halves(matrix))
    return np.stack(found)


def along_y_matrix():
    scale = -sharpness / math.log(2.0)
    main = np.zeros((512, 256))
    for out in range(256):
        for distance in range(-4, 5):
            main[128 + out + distance, out] = scale * tap(distance)
    return halves(main)[:, BAND[0] : BAND[1]]


MEAN = np.array([0, 1, 1, 1, 1, 0]) / 4
FIRST = np.array([0, 1, 0, 0, 0, 0]) / 1
SOFT = np.array([1, 3, 4, 4, 3, 1]) / 16
SLOPE = np.array([-1, -1, 0, 0, 1, 1]) / 8


def cell_matrices():
    pairs = [(MEAN, MEAN), (FIRST, MEAN), (MEAN, FIRST), (SLOPE, SOFT), (SOFT, SLOPE), (SOFT, SOFT)]
    inner = np.zeros((len(pairs) * ROWS, GROUPS * INNER))
    outer = np.zeros((len(pairs) * ROWS, GROUPS * OUTER))
    for at, (along_z, along_x) in enumerate(pairs):
        for layer in range(4):
            for cell in range(8):
                for z in range(6):
                    for x in range(6):
                        group, plane = divmod(4 * layer + z, GROUP_PLANES)
                        row = row_of(plane, 4 * cell + x)
                        out = at * ROWS + layer * 8 + cell
                        weight = along_z[z] * along_x[x]
                        if row < INNER:
                            inner[out, group * INNER + row] += weight
                        else:
                            outer[out, group * OUTER + row - INNER] += weight
    return inner.astype(ml_dtypes.bfloat16), outer.astype(ml_dtypes.bfloat16)


def cell_y_matrix():
    matrix = np.zeros((2, TILE_Y + 128, 256))
    for at, weights in enumerate((MEAN, FIRST, SOFT, SLOPE)):
        for cell in range(128):
            for y in range(6):
                place = 4 * cell + y - 1
                row = TILE_Y + 127 if place < 0 else place
                matrix[at // 2, row, at % 2 * 128 + cell] = weights[y]
    return matrix.astype(ml_dtypes.bfloat16)


def side_marks():
    marks = np.zeros((8, GROUPS * OUTER), np.float32)
    for group in range(GROUPS):
        for plane in range(GROUP_PLANES):
            marks[0, group * OUTER + plane * OUTER_X] = 1
            marks[1, group * OUTER + plane * OUTER_X + OUTER_X - 1] = 1
    return marks


def split(value):
    high = value.astype(jnp.bfloat16)
    return high, (value - high.astype(jnp.float32)).astype(jnp.bfloat16)


def dot(left, right):
    return jnp.dot(left, right, preferred_element_type=jnp.float32)


def routing(owner, flags):
    wide = (ROWS, ROWS)
    row = lax.broadcasted_iota(jnp.int32, wide, 0)
    column = lax.broadcasted_iota(jnp.int32, wide, 1)
    owner_across = jnp.broadcast_to(owner.astype(jnp.float32), wide)
    flag_across = jnp.broadcast_to(flags.astype(jnp.float32), wide)
    same = row == column
    owner_down = jnp.sum(jnp.where(same, owner_across, 0.0), axis=1, keepdims=True)
    flag_down = jnp.sum(jnp.where(same, flag_across, 0.0), axis=1, keepdims=True)
    earlier = (column < row) & (owner_down == owner_across)
    slot = jnp.sum(jnp.where(earlier, flag_across, 0.0), axis=1, keepdims=True)
    code = jnp.where(flag_down > 0.5, owner_down * 2.0 + slot, -8.0)
    place = lax.broadcasted_iota(jnp.int32, (ROWS, 256), 1)
    mine = (place & (ROWS - 1)) == lax.broadcasted_iota(jnp.int32, (ROWS, 256), 0)
    spread = jnp.sum(jnp.where(mine, code, 0.0), axis=0, keepdims=True)
    part = ((lax.broadcasted_iota(jnp.int32, (1, 256), 1) >> 5) & 3).astype(jnp.float32)
    return spread * 4.0 + part


def kernel(
    count_x, count_y,
    volume, owner_h, flags_h, marks_h,
    take_w, pack_w, own_w, main_w, put_w, inner_w, side_w, outer_w, cell_y_w,
    geometry_h, arrived,
    tile, packed, columns, corners, sides, beside, corner_in, ends, side_ends,
    smooth, sharp, chosen, leaving, geometry, owner, flags, marks, main_v,
    take_v, pack_v, own_v, put_v, inner_v, side_v, outer_v, cell_y_v,
    load_sem, send_sem, recv_sem, far_sem, out_send, out_recv, own_sem, geometry_sem,
):
    p = lax.axis_index("gx")
    q = lax.axis_index("gy")
    count = count_x * count_y
    me = p * count_y + q

    def at(dx, dy):
        return (lax.rem(p + dx + count_x, count_x), lax.rem(q + dy + count_y, count_y))

    around = [(0, -1), (0, 1), (-1, 0), (1, 0), (-1, -1), (-1, 1), (1, -1), (1, 1)]
    barrier = pltpu.get_barrier_semaphore()
    for dx, dy in around:
        pl.semaphore_signal(barrier, inc=1, device_id=at(dx, dy), device_id_type=MESH)
    pairs = [
        (volume, tile),
        (pack_w, pack_v),
        (take_w, take_v),
        (own_w, own_v),
        (owner_h, owner),
        (flags_h, flags),
        (put_w, put_v),
        (main_w, main_v.at[:, pl.ds(BAND[0], BAND[1] - BAND[0]), :]),
        (inner_w, inner_v),
        (side_w, side_v),
        (marks_h, marks),
        (outer_w, outer_v),
        (cell_y_w, cell_y_v),
    ]
    loads = [pltpu.make_async_copy(*pair, load_sem.at[i]) for i, pair in enumerate(pairs)]
    for load in loads[0:4]:
        load.start()
    main_v[:, 0 : BAND[0], :] = jnp.zeros((2, BAND[0], 256), jnp.bfloat16)
    main_v[:, BAND[1] : 512, :] = jnp.zeros((2, 512 - BAND[1], 256), jnp.bfloat16)

    def take_columns(rows):
        both = jnp.concatenate([rows[:, 0:128], rows[:, TILE_Y - 128 : TILE_Y]], axis=1)
        return lax.dot_general(
            take_v[...], both, (((1,), (1,)), ((), ())), preferred_element_type=jnp.float32
        ).astype(jnp.bfloat16)

    def put_columns(taken):
        return lax.dot_general(
            taken, put_v[...], (((0,), (0,)), ((), ())), preferred_element_type=jnp.float32
        ).astype(jnp.bfloat16)

    for load in loads[0:3]:
        load.wait()
    for load in loads[4:]:
        load.start()
    own = tile[...].reshape(OWN, TILE_Y)
    low_rows, high_rows = [], []
    for first in range(0, PLANES_IN, PACK_PLANES):
        block = own[first * TILE_X : min(first + PACK_PLANES, PLANES_IN) * TILE_X]
        taken = dot(pack_v[:, 0 : block.shape[0]], block)
        rows = min(PACK_ROWS, SIDE_ROWS - first * REACH)
        low_rows.append(taken[0:rows])
        high_rows.append(taken[PACK_ROWS : PACK_ROWS + rows])
    edge_rows = jnp.concatenate(low_rows + high_rows, axis=0).astype(jnp.bfloat16)
    packed[...] = edge_rows
    columns[:, 0:OWN] = take_columns(own)
    for side in range(2):
        corners[side, :, 0:SIDE_ROWS] = take_columns(
            edge_rows[side * SIDE_ROWS : (side + 1) * SIDE_ROWS]
        )

    pl.semaphore_wait(barrier, len(around))
    diagonals = around[4:]
    for dx, dy in diagonals:
        pl.semaphore_signal(far_sem.at[0], inc=1, device_id=at(dx, dy), device_id_type=MESH)
    sends = []
    for i, (dx, dy) in enumerate(around):
        rows, rows_there = (0, SIDE_ROWS) if dx < 0 else (SIDE_ROWS, 0)
        lines, lines_there = (0, 16) if dy < 0 else (16, 0)
        if dx == 0:
            source = columns.at[pl.ds(lines, 16), :]
            target = beside.at[pl.ds(lines_there, 16), :]
        elif dy == 0:
            source = packed.at[pl.ds(rows, SIDE_ROWS), :]
            target = sides.at[pl.ds(rows_there, SIDE_ROWS), :]
        else:
            source = corners.at[rows // SIDE_ROWS, pl.ds(lines, 16), :]
            target = corner_in.at[rows_there // SIDE_ROWS, pl.ds(lines_there, 16), :]
        sends.append(
            pltpu.make_async_remote_copy(
                src_ref=source,
                dst_ref=target,
                send_sem=send_sem.at[i],
                recv_sem=recv_sem.at[i],
                device_id=at(dx, dy),
                device_id_type=MESH,
            )
        )
    for send in sends:
        send.start()

    loads[3].wait()
    for g in range(GROUPS):
        block = tile[g * GROUP_PLANES : g * GROUP_PLANES + GROUP_IN].reshape(
            GROUP_IN * TILE_X, TILE_Y
        )
        smooth[g, :, 128:WIDE_Y] = dot(own_v[0], block) + dot(own_v[1], block)

    for load in loads[4:6]:
        load.wait()
    codes = routing(owner[...], flags[...])
    number = lax.broadcasted_iota(jnp.int32, (count * 8, 256), 0).astype(jnp.float32)
    chosen[...] = jnp.where(number == codes, 1.0, 0.0).astype(jnp.bfloat16)

    pl.semaphore_wait(far_sem.at[0], len(diagonals))
    for dx, dy in diagonals:
        pl.semaphore_signal(
            far_sem.at[1], inc=1, device_id=at(2 * dx, 2 * dy), device_id_type=MESH
        )
    for load in loads[6:]:
        load.wait()
    for send in sends[0:2]:
        send.wait()

    @pl.when(q == 0)
    def _():
        beside[0:16, :] = jnp.zeros((16, beside.shape[1]), jnp.bfloat16)

    @pl.when(q == count_y - 1)
    def _():
        beside[16:32, :] = jnp.zeros((16, beside.shape[1]), jnp.bfloat16)

    lane = lax.broadcasted_iota(jnp.int32, (1, 128), 1)
    left_out = jnp.where(q == 0, 127, -1)
    right_out = jnp.where(q == count_y - 1, 0, -1)
    edge_keep = jnp.where((lane == left_out) | (lane == right_out), 0.0, 1.0)

    def sigmoid_of(power):
        below = 1.0 + jnp.exp2(jnp.minimum(power, 126.0))
        guess = pl.reciprocal(below, approx=True)
        return guess * (2.0 - below * guess)

    def indicator(blurred):
        high, low = split(blurred)

        def along_y(choose, weights):
            high_part = choose(high)
            return (
                dot(high_part, weights[0])
                + dot(choose(low), weights[0])
                + dot(high_part, weights[1])
            )

        def last(part):
            return jnp.concatenate([part[:, 256:WIDE_Y], part[:, 0:128]], axis=1)

        def right_end(part):
            return jnp.concatenate([part[:, 512:WIDE_Y], part[:, 0:128]], axis=1)

        left = along_y(lambda part: part[:, 0:256], main_v[:, 128:384, 0:128])
        right = along_y(right_end, main_v[:, 128:384, 128:256])
        edge = jnp.where(lane == 127, left, right)
        return split(
            jnp.concatenate(
                [
                    sigmoid_of(along_y(lambda part: part[:, 0:512], main_v[...])),
                    sigmoid_of(along_y(last, main_v[...])),
                    edge_keep * sigmoid_of(edge),
                ],
                axis=1,
            )
        )

    ends[...] = put_columns(beside[:, 0:OWN])
    for g in range(GROUPS):
        first = g * GROUP_PLANES * TILE_X
        block = ends[first : first + GROUP_IN * TILE_X, :]
        smooth[g, :, 0:128] = dot(own_v[0], block) + dot(own_v[1], block)
        high, low = indicator(smooth[g, 0:INNER, :])
        sharp[0, g * INNER : (g + 1) * INNER, :] = high
        sharp[1, g * INNER : (g + 1) * INNER, :] = low
    cells = dot(inner_v[...], sharp[0]) + dot(inner_v[...], sharp[1])

    pl.semaphore_wait(far_sem.at[1], len(diagonals))
    for dx in (-4, 4):
        pl.semaphore_signal(far_sem.at[2], inc=1, device_id=at(dx, 0), device_id_type=MESH)
    for send in sends[2:]:
        send.wait()

    @pl.when(p == 0)
    def _():
        sides[0:SIDE_ROWS, :] = jnp.zeros((SIDE_ROWS, TILE_Y), jnp.bfloat16)
        corner_in[0] = jnp.zeros(corner_in.shape[1:], jnp.bfloat16)

    @pl.when(p == count_x - 1)
    def _():
        sides[SIDE_ROWS : 2 * SIDE_ROWS, :] = jnp.zeros((SIDE_ROWS, TILE_Y), jnp.bfloat16)
        corner_in[1] = jnp.zeros(corner_in.shape[1:], jnp.bfloat16)

    @pl.when(q == 0)
    def _():
        corner_in[:, 0:16, :] = jnp.zeros((2, 16, corner_in.shape[2]), jnp.bfloat16)

    @pl.when(q == count_y - 1)
    def _():
        corner_in[:, 16:32, :] = jnp.zeros((2, 16, corner_in.shape[2]), jnp.bfloat16)

    for side in range(2):
        side_ends[side * SIDE_ROWS : (side + 1) * SIDE_ROWS, :] = put_columns(
            corner_in[side, :, 0:SIDE_ROWS]
        )
    blurred = []
    for g in range(GROUPS):
        low_rows = slice(WINDOW_AT[g], WINDOW_AT[g] + WINDOW)
        high_rows = slice(SIDE_ROWS + WINDOW_AT[g], SIDE_ROWS + WINDOW_AT[g] + WINDOW)
        window = jnp.concatenate(
            [
                jnp.concatenate([side_ends[low_rows, :], sides[low_rows, :]], axis=1),
                jnp.concatenate([side_ends[high_rows, :], sides[high_rows, :]], axis=1),
            ],
            axis=0,
        )
        blurred.append(
            dot(side_v[g, 0], window) + dot(side_v[g, 1], window) + smooth[g, INNER:GROUP_ROWS, :]
        )
    high, low = indicator(jnp.concatenate(blurred, axis=0))
    low_out = jnp.where(p == 0, 1.0, 0.0)
    high_out = jnp.where(p == count_x - 1, 1.0, 0.0)
    keep = (1.0 - low_out * marks[0:1, :] - high_out * marks[1:2, :]).astype(jnp.bfloat16)
    weights = outer_v[...] * keep
    cells = cells + dot(weights, high) + dot(weights, low)

    high, low = split(cells)
    plain = dot(high[0:96], cell_y_v[0]) + dot(low[0:96], cell_y_v[0])
    slopes = dot(high[96:192], cell_y_v[1]) + dot(low[96:192], cell_y_v[1])
    mean_z, mean_x, mean_y = slopes[0:32, 0:128], slopes[32:64, 0:128], slopes[64:96, 128:256]
    shrink = -lax.rsqrt(mean_z * mean_z + mean_x * mean_x + mean_y * mean_y + normal_floor)
    found = [
        plain[0:32, 0:128],
        plain[32:64, 0:128],
        plain[64:96, 0:128],
        plain[0:32, 128:256],
        mean_z * shrink,
        mean_x * shrink,
        mean_y * shrink,
    ]
    for channel in range(CHANNELS):
        geometry[channel] = found[channel]
    write = pltpu.make_async_copy(geometry, geometry_h, geometry_sem)
    write.start()

    most = functools.reduce(jnp.maximum, [jnp.abs(value) for value in found])
    most = jnp.maximum(jnp.max(most, axis=1, keepdims=True), 1e-37)
    grade = jnp.ceil(8.0 * jnp.log2(most) + 0.02)
    stretch = jnp.exp2(grade * -0.125)
    whole = [jnp.floor(value * stretch * LEVELS + 0.5) for value in found]
    whole.append(jnp.broadcast_to(grade, (ROWS, 128)))
    coded = jnp.concatenate(
        [jnp.concatenate(whole[0:4], axis=0), jnp.concatenate(whole[4:8], axis=0)], axis=1
    )
    upper = jnp.floor(coded * (1.0 / 256.0) + 0.5) * 256.0
    stacked = jnp.concatenate([upper, coded - upper], axis=0).astype(jnp.bfloat16)
    placed = dot(chosen[...], stacked).astype(jnp.int32)
    joined = (placed[:, 128:256] << 16) | (placed[:, 0:128] & 0xFFFF)
    leaving[...] = joined.reshape(count, 8, 128)

    pl.semaphore_wait(far_sem.at[2], 2)

    def send_out(step, carry):
        other = lax.rem(me + step, count)
        pltpu.make_async_remote_copy(
            src_ref=leaving.at[other],
            dst_ref=arrived.at[me],
            send_sem=out_send,
            recv_sem=out_recv,
            device_id=(other // count_y, lax.rem(other, count_y)),
            device_id_type=MESH,
        ).start()
        return carry

    lax.fori_loop(1, count, send_out, 0)
    stay = pltpu.make_async_copy(leaving.at[me], arrived.at[me], own_sem)
    stay.start()
    others = pl.ds(0, count - 1)
    every = pltpu.make_async_remote_copy(
        src_ref=leaving.at[others],
        dst_ref=arrived.at[others],
        send_sem=out_send,
        recv_sem=out_recv,
        device_id=at(1, 0),
        device_id_type=MESH,
    )
    every.wait_send()
    every.wait_recv()
    stay.wait()
    write.wait()


def decode_kernel(
    coded, geometry_in, received, geometry, coded_v, geometry_v, received_v,
    copy_sem, load_sem, store_sem,
):
    pieces = load_sem.shape[0]
    rows = received_v.shape[1] // pieces
    whole_in = pltpu.make_async_copy(geometry_in, geometry_v, copy_sem.at[0])
    whole_out = pltpu.make_async_copy(geometry_v, geometry, copy_sem.at[1])
    loads, stores = [], []
    for i in range(pieces):
        source = pl.ds(i * rows * 4, rows * 4)
        target = pl.ds(i * rows, rows)
        loads.append(
            pltpu.make_async_copy(coded.at[source, :], coded_v.at[source, :], load_sem.at[i])
        )
        stores.append(
            pltpu.make_async_copy(
                received_v.at[:, target, :], received.at[:, target, :], store_sem.at[i]
            )
        )
    for load in loads:
        load.start()
    whole_in.start()
    for i in range(pieces):
        loads[i].wait()
        target = slice(i * rows, (i + 1) * rows)

        def pair(part):
            both = coded_v[pl.ds(i * rows * 4 + part, rows, stride=4), :]
            return (both << 16) >> 16, both >> 16

        fourth, grade = pair(3)
        scale = jnp.exp2(grade.astype(jnp.float32) * 0.125) * (1.0 / LEVELS)
        received_v[3, target] = fourth.astype(jnp.float32) * scale
        for part in range(3):
            low, high = pair(part)
            received_v[part, target] = low.astype(jnp.float32) * scale
            received_v[part + 4, target] = high.astype(jnp.float32) * scale
        stores[i].start()
    whole_in.wait()
    whole_out.start()
    for store in stores:
        store.wait()
    whole_out.wait()


def body(count_x, count_y, volume, owner, flags):
    count = count_x * count_y
    inner_w, outer_w = cell_matrices()
    take_w, put_w = column_matrices()
    weights = [
        take_w, pack_matrix(), own_matrix(), along_y_matrix(), put_w, inner_w, side_matrices(), outer_w, cell_y_matrix(),
    ]
    anywhere = pl.BlockSpec(memory_space=pl.ANY)
    bf16 = jnp.bfloat16
    marks = side_marks()
    geometry, arrived = pl.pallas_call(
        functools.partial(kernel, count_x, count_y),
        out_shape=(
            jax.ShapeDtypeStruct((CHANNELS, ROWS, 128), jnp.float32),
            jax.ShapeDtypeStruct((count, 8, 128), jnp.int32),
        ),
        in_specs=[anywhere] * (4 + len(weights)),
        out_specs=(anywhere, anywhere),
        scratch_shapes=[
            pltpu.VMEM((PLANES_IN, TILE_X, TILE_Y), bf16),
            pltpu.VMEM((2 * SIDE_ROWS, TILE_Y), bf16),
            pltpu.VMEM((32, 896), bf16),
            pltpu.VMEM((2, 32, 256), bf16),
            pltpu.VMEM((2 * SIDE_ROWS, TILE_Y), bf16),
            pltpu.VMEM((32, 896), bf16),
            pltpu.VMEM((2, 32, 256), bf16),
            pltpu.VMEM((OWN, 128), bf16),
            pltpu.VMEM((2 * SIDE_ROWS, 128), bf16),
            pltpu.VMEM((GROUPS, GROUP_ROWS, WIDE_Y), jnp.float32),
            pltpu.VMEM((2, GROUPS * INNER, WIDE_Y), bf16),
            pltpu.VMEM((count * 8, 256), bf16),
            pltpu.VMEM((count, 8, 128), jnp.int32),
            pltpu.VMEM((CHANNELS, ROWS, 128), jnp.float32),
            pltpu.VMEM((1, ROWS), jnp.int32),
            pltpu.VMEM((1, ROWS), jnp.int32),
            pltpu.VMEM(marks.shape, jnp.float32),
            pltpu.VMEM((2, 512, 256), bf16),
        ]
        + [pltpu.VMEM(weight.shape, bf16) for weight in weights if weight is not weights[3]]
        + [
            pltpu.SemaphoreType.DMA((4 + len(weights),)),
            pltpu.SemaphoreType.DMA((8,)),
            pltpu.SemaphoreType.DMA((8,)),
            pltpu.SemaphoreType.REGULAR((3,)),
            pltpu.SemaphoreType.DMA,
            pltpu.SemaphoreType.DMA,
            pltpu.SemaphoreType.DMA,
            pltpu.SemaphoreType.DMA,
        ],
        compiler_params=pltpu.CompilerParams(
            collective_id=0, has_side_effects=True, vmem_limit_bytes=62 * 2**20
        ),
    )(volume, owner.reshape(1, ROWS), flags.reshape(1, ROWS), marks, *weights)
    pieces = 4
    received, geometry = pl.pallas_call(
        decode_kernel,
        out_shape=(
            jax.ShapeDtypeStruct((CHANNELS, count * 2, 128), jnp.float32),
            jax.ShapeDtypeStruct(geometry.shape, jnp.float32),
        ),
        in_specs=[anywhere, anywhere],
        out_specs=(anywhere, anywhere),
        scratch_shapes=[
            pltpu.VMEM((count * 8, 128), jnp.int32),
            pltpu.VMEM(geometry.shape, jnp.float32),
            pltpu.VMEM((CHANNELS, count * 2, 128), jnp.float32),
            pltpu.SemaphoreType.DMA((2,)),
            pltpu.SemaphoreType.DMA((pieces,)),
            pltpu.SemaphoreType.DMA((pieces,)),
        ],
        compiler_params=pltpu.CompilerParams(vmem_limit_bytes=62 * 2**20),
    )(arrived.reshape(count * 8, 128), geometry)
    received = jnp.transpose(received, (1, 0, 2))[None]
    return (geometry.reshape(CHANNELS, 4, 8, 128), received)


def solution(mesh):
    in_specs = (P(None, "gx", "gy"), P("gx", "gy", None, None), P("gx", "gy", None))
    out_specs = (P(None, None, "gx", "gy"), P(("gx", "gy"), None, None, None))
    return jax.shard_map(
        functools.partial(body, mesh.shape["gx"], mesh.shape["gy"]),
        mesh=mesh,
        in_specs=in_specs,
        out_specs=out_specs,
        check_vma=False,
    )
```

```python
import functools
import math

import jax
import jax.numpy as jnp
import ml_dtypes
import numpy as np
from jax import lax
from jax.experimental import pallas as pl
from jax.experimental.pallas import tpu as pltpu
from jax.sharding import PartitionSpec as P

MESH = pl.DeviceIdType.MESH

raw_taps = [math.exp(-((offset - 4) ** 2) / 8.0) for offset in range(9)]
gauss_taps = np.array([value / sum(raw_taps) for value in raw_taps])
sharpness = 20.0
normal_floor = 0.01

PLANES_IN = 26
TILE_X = 32
TILE_Y = 512
OWN = PLANES_IN * TILE_X
REACH = 5
WIDE_X = TILE_X + 2
GROUPS = 3
GROUP_PLANES = 6
GROUP_IN = GROUP_PLANES + 8
INNER_X = 24
OUTER_X = 10
INNER = GROUP_PLANES * INNER_X
OUTER = 64
GROUP_ROWS = INNER + OUTER
SIDE_ROWS = 144
WINDOW = 96
WINDOW_AT = [(REACH * GROUP_PLANES * g) // 16 * 16 for g in range(GROUPS)]
PACK_PLANES = 8
PACK_ROWS = PACK_PLANES * REACH
WIDE_Y = TILE_Y + 128
BAND = (112, 400)
ROWS = 32
CHANNELS = 7
LEVELS = 32766.0


def outer_place(x):
    if x < REACH:
        return x
    return x - INNER_X if x >= REACH + INNER_X else None


def row_of(plane, x):
    outer = outer_place(x)
    if outer is None:
        return plane * INNER_X + x - REACH
    return INNER + plane * OUTER_X + outer


def halves(matrix):
    high = matrix.astype(np.float32).astype(ml_dtypes.bfloat16)
    low = (matrix - high.astype(np.float64)).astype(np.float32).astype(ml_dtypes.bfloat16)
    return np.stack([high, low])


def pack_matrix():
    matrix = np.zeros((2 * PACK_ROWS, PACK_PLANES * TILE_X))
    for z in range(PACK_PLANES):
        for i in range(REACH):
            matrix[z * REACH + i, z * TILE_X + i] = 1
            matrix[PACK_ROWS + z * REACH + i, z * TILE_X + TILE_X - REACH + i] = 1
    return matrix.astype(ml_dtypes.bfloat16)


def column_matrices():
    take = np.zeros((32, 256))
    put = np.zeros((32, 128))
    for i in range(REACH):
        take[i, i] = 1
        take[16 + i, 256 - REACH + i] = 1
        put[i, 128 - REACH + i] = 1
        put[16 + i, i] = 1
    return take.astype(ml_dtypes.bfloat16), put.astype(ml_dtypes.bfloat16)


def tap(distance):
    return gauss_taps[distance + 4] if -4 <= distance <= 4 else 0.0


def own_matrix():
    matrix = np.zeros((GROUP_ROWS, GROUP_IN * TILE_X))
    for plane in range(GROUP_PLANES):
        for x in range(WIDE_X):
            for z in range(9):
                for source in range(TILE_X):
                    matrix[row_of(plane, x), (plane + z) * TILE_X + source] = (
                        gauss_taps[z] * tap(source - (x - 1))
                    )
    return halves(matrix)


def side_matrices():
    found = []
    for g in range(GROUPS):
        matrix = np.zeros((OUTER, 2 * WINDOW))
        for plane in range(GROUP_PLANES):
            for x in range(WIDE_X):
                outer = outer_place(x)
                if outer is None:
                    continue
                for z in range(9):
                    for i in range(REACH):
                        row = (g * GROUP_PLANES + plane + z) * REACH + i - WINDOW_AT[g]
                        out = plane * OUTER_X + outer
                        matrix[out, row] = gauss_taps[z] * tap(i - REACH - (x - 1))
                        matrix[out, WINDOW + row] = gauss_taps[z] * tap(TILE_X + i - (x - 1))
        found.append(halves(matrix))
    return np.stack(found)


def along_y_matrix():
    scale = -sharpness / math.log(2.0)
    main = np.zeros((512, 256))
    for out in range(256):
        for distance in range(-4, 5):
            main[128 + out + distance, out] = scale * tap(distance)
    return halves(main)[:, BAND[0] : BAND[1]]


MEAN = np.array([0, 1, 1, 1, 1, 0]) / 4
FIRST = np.array([0, 1, 0, 0, 0, 0]) / 1
SOFT = np.array([1, 3, 4, 4, 3, 1]) / 16
SLOPE = np.array([-1, -1, 0, 0, 1, 1]) / 8


def cell_matrices():
    pairs = [(MEAN, MEAN), (FIRST, MEAN), (MEAN, FIRST), (SLOPE, SOFT), (SOFT, SLOPE), (SOFT, SOFT)]
    inner = np.zeros((len(pairs) * ROWS, GROUPS * INNER))
    outer = np.zeros((len(pairs) * ROWS, GROUPS * OUTER))
    for at, (along_z, along_x) in enumerate(pairs):
        for layer in range(4):
            for cell in range(8):
                for z in range(6):
                    for x in range(6):
                        group, plane = divmod(4 * layer + z, GROUP_PLANES)
                        row = row_of(plane, 4 * cell + x)
                        out = at * ROWS + layer * 8 + cell
                        weight = along_z[z] * along_x[x]
                        if row < INNER:
                            inner[out, group * INNER + row] += weight
                        else:
                            outer[out, group * OUTER + row - INNER] += weight
    return inner.astype(ml_dtypes.bfloat16), outer.astype(ml_dtypes.bfloat16)


def cell_y_matrix():
    matrix = np.zeros((2, TILE_Y + 128, 256))
    for at, weights in enumerate((MEAN, FIRST, SOFT, SLOPE)):
        for cell in range(128):
            for y in range(6):
                place = 4 * cell + y - 1
                row = TILE_Y + 127 if place < 0 else place
                matrix[at // 2, row, at % 2 * 128 + cell] = weights[y]
    return matrix.astype(ml_dtypes.bfloat16)


def side_marks():
    marks = np.zeros((8, GROUPS * OUTER), np.float32)
    for group in range(GROUPS):
        for plane in range(GROUP_PLANES):
            marks[0, group * OUTER + plane * OUTER_X] = 1
            marks[1, group * OUTER + plane * OUTER_X + OUTER_X - 1] = 1
    return marks


def split(value):
    high = value.astype(jnp.bfloat16)
    return high, (value - high.astype(jnp.float32)).astype(jnp.bfloat16)


def dot(left, right):
    return jnp.dot(left, right, preferred_element_type=jnp.float32)


def routing(owner, flags):
    wide = (ROWS, ROWS)
    row = lax.broadcasted_iota(jnp.int32, wide, 0)
    column = lax.broadcasted_iota(jnp.int32, wide, 1)
    owner_across = jnp.broadcast_to(owner.astype(jnp.float32), wide)
    flag_across = jnp.broadcast_to(flags.astype(jnp.float32), wide)
    same = row == column
    owner_down = jnp.sum(jnp.where(same, owner_across, 0.0), axis=1, keepdims=True)
    flag_down = jnp.sum(jnp.where(same, flag_across, 0.0), axis=1, keepdims=True)
    earlier = (column < row) & (owner_down == owner_across)
    slot = jnp.sum(jnp.where(earlier, flag_across, 0.0), axis=1, keepdims=True)
    code = jnp.where(flag_down > 0.5, owner_down * 2.0 + slot, -8.0)
    place = lax.broadcasted_iota(jnp.int32, (ROWS, 256), 1)
    mine = (place & (ROWS - 1)) == lax.broadcasted_iota(jnp.int32, (ROWS, 256), 0)
    spread = jnp.sum(jnp.where(mine, code, 0.0), axis=0, keepdims=True)
    part = ((lax.broadcasted_iota(jnp.int32, (1, 256), 1) >> 5) & 3).astype(jnp.float32)
    return spread * 4.0 + part


def kernel(
    count_x, count_y,
    volume, owner_h, flags_h, marks_h,
    take_w, pack_w, own_w, main_w, put_w, inner_w, side_w, outer_w, cell_y_w,
    geometry_h, arrived,
    tile, packed, columns, corners, sides, beside, corner_in, ends, side_ends,
    smooth, sharp, chosen, leaving, geometry, owner, flags, marks, main_v,
    take_v, pack_v, own_v, put_v, inner_v, side_v, outer_v, cell_y_v,
    load_sem, send_sem, recv_sem, far_sem, out_send, out_recv, own_sem, geometry_sem,
):
    p = lax.axis_index("gx")
    q = lax.axis_index("gy")
    count = count_x * count_y
    me = p * count_y + q

    def at(dx, dy):
        return (lax.rem(p + dx + count_x, count_x), lax.rem(q + dy + count_y, count_y))

    around = [(0, -1), (0, 1), (-1, 0), (1, 0), (-1, -1), (-1, 1), (1, -1), (1, 1)]
    barrier = pltpu.get_barrier_semaphore()
    for dx, dy in around:
        pl.semaphore_signal(barrier, inc=1, device_id=at(dx, dy), device_id_type=MESH)
    pairs = [
        (volume, tile),
        (pack_w, pack_v),
        (take_w, take_v),
        (own_w, own_v),
        (owner_h, owner),
        (flags_h, flags),
        (put_w, put_v),
        (main_w, main_v.at[:, pl.ds(BAND[0], BAND[1] - BAND[0]), :]),
        (inner_w, inner_v),
        (side_w, side_v),
        (marks_h, marks),
        (outer_w, outer_v),
        (cell_y_w, cell_y_v),
    ]
    loads = [pltpu.make_async_copy(*pair, load_sem.at[i]) for i, pair in enumerate(pairs)]
    for load in loads[0:4]:
        load.start()
    main_v[:, 0 : BAND[0], :] = jnp.zeros((2, BAND[0], 256), jnp.bfloat16)
    main_v[:, BAND[1] : 512, :] = jnp.zeros((2, 512 - BAND[1], 256), jnp.bfloat16)

    def take_columns(rows):
        both = jnp.concatenate([rows[:, 0:128], rows[:, TILE_Y - 128 : TILE_Y]], axis=1)
        return lax.dot_general(
            take_v[...], both, (((1,), (1,)), ((), ())), preferred_element_type=jnp.float32
        ).astype(jnp.bfloat16)

    def put_columns(taken):
        return lax.dot_general(
            taken, put_v[...], (((0,), (0,)), ((), ())), preferred_element_type=jnp.float32
        ).astype(jnp.bfloat16)

    for load in loads[0:3]:
        load.wait()
    for load in loads[4:]:
        load.start()
    own = tile[...].reshape(OWN, TILE_Y)
    low_rows, high_rows = [], []
    for first in range(0, PLANES_IN, PACK_PLANES):
        block = own[first * TILE_X : min(first + PACK_PLANES, PLANES_IN) * TILE_X]
        taken = dot(pack_v[:, 0 : block.shape[0]], block)
        rows = min(PACK_ROWS, SIDE_ROWS - first * REACH)
        low_rows.append(taken[0:rows])
        high_rows.append(taken[PACK_ROWS : PACK_ROWS + rows])
    edge_rows = jnp.concatenate(low_rows + high_rows, axis=0).astype(jnp.bfloat16)
    packed[...] = edge_rows
    columns[:, 0:OWN] = take_columns(own)
    for side in range(2):
        corners[side, :, 0:SIDE_ROWS] = take_columns(
            edge_rows[side * SIDE_ROWS : (side + 1) * SIDE_ROWS]
        )

    pl.semaphore_wait(barrier, len(around))
    diagonals = around[4:]
    for dx, dy in diagonals:
        pl.semaphore_signal(far_sem.at[0], inc=1, device_id=at(dx, dy), device_id_type=MESH)
    sends = []
    for i, (dx, dy) in enumerate(around):
        rows, rows_there = (0, SIDE_ROWS) if dx < 0 else (SIDE_ROWS, 0)
        lines, lines_there = (0, 16) if dy < 0 else (16, 0)
        if dx == 0:
            source = columns.at[pl.ds(lines, 16), :]
            target = beside.at[pl.ds(lines_there, 16), :]
        elif dy == 0:
            source = packed.at[pl.ds(rows, SIDE_ROWS), :]
            target = sides.at[pl.ds(rows_there, SIDE_ROWS), :]
        else:
            source = corners.at[rows // SIDE_ROWS, pl.ds(lines, 16), :]
            target = corner_in.at[rows_there // SIDE_ROWS, pl.ds(lines_there, 16), :]
        sends.append(
            pltpu.make_async_remote_copy(
                src_ref=source,
                dst_ref=target,
                send_sem=send_sem.at[i],
                recv_sem=recv_sem.at[i],
                device_id=at(dx, dy),
                device_id_type=MESH,
            )
        )
    for send in sends:
        send.start()

    loads[3].wait()
    for g in range(GROUPS):
        block = tile[g * GROUP_PLANES : g * GROUP_PLANES + GROUP_IN].reshape(
            GROUP_IN * TILE_X, TILE_Y
        )
        smooth[g, :, 128:WIDE_Y] = dot(own_v[0], block) + dot(own_v[1], block)

    for load in loads[4:6]:
        load.wait()
    codes = routing(owner[...], flags[...])
    number = lax.broadcasted_iota(jnp.int32, (count * 8, 256), 0).astype(jnp.float32)
    chosen[...] = jnp.where(number == codes, 1.0, 0.0).astype(jnp.bfloat16)

    pl.semaphore_wait(far_sem.at[0], len(diagonals))
    for dx, dy in diagonals:
        pl.semaphore_signal(
            far_sem.at[1], inc=1, device_id=at(2 * dx, 2 * dy), device_id_type=MESH
        )
    for load in loads[6:]:
        load.wait()
    for send in sends[0:2]:
        send.wait()

    @pl.when(q == 0)
    def _():
        beside[0:16, :] = jnp.zeros((16, beside.shape[1]), jnp.bfloat16)

    @pl.when(q == count_y - 1)
    def _():
        beside[16:32, :] = jnp.zeros((16, beside.shape[1]), jnp.bfloat16)

    lane = lax.broadcasted_iota(jnp.int32, (1, 128), 1)
    left_out = jnp.where(q == 0, 127, -1)
    right_out = jnp.where(q == count_y - 1, 0, -1)
    edge_keep = jnp.where((lane == left_out) | (lane == right_out), 0.0, 1.0)

    def sigmoid_of(power):
        below = 1.0 + jnp.exp2(jnp.minimum(power, 126.0))
        guess = pl.reciprocal(below, approx=True)
        return guess * (2.0 - below * guess)

    def indicator(blurred):
        high, low = split(blurred)

        def along_y(choose, weights):
            high_part = choose(high)
            return (
                dot(high_part, weights[0])
                + dot(choose(low), weights[0])
                + dot(high_part, weights[1])
            )

        def last(part):
            return jnp.concatenate([part[:, 256:WIDE_Y], part[:, 0:128]], axis=1)

        def right_end(part):
            return jnp.concatenate([part[:, 512:WIDE_Y], part[:, 0:128]], axis=1)

        left = along_y(lambda part: part[:, 0:256], main_v[:, 128:384, 0:128])
        right = along_y(right_end, main_v[:, 128:384, 128:256])
        edge = jnp.where(lane == 127, left, right)
        return split(
            jnp.concatenate(
                [
                    sigmoid_of(along_y(lambda part: part[:, 0:512], main_v[...])),
                    sigmoid_of(along_y(last, main_v[...])),
                    edge_keep * sigmoid_of(edge),
                ],
                axis=1,
            )
        )

    ends[...] = put_columns(beside[:, 0:OWN])
    for g in range(GROUPS):
        first = g * GROUP_PLANES * TILE_X
        block = ends[first : first + GROUP_IN * TILE_X, :]
        smooth[g, :, 0:128] = dot(own_v[0], block) + dot(own_v[1], block)
        high, low = indicator(smooth[g, 0:INNER, :])
        sharp[0, g * INNER : (g + 1) * INNER, :] = high
        sharp[1, g * INNER : (g + 1) * INNER, :] = low
    cells = dot(inner_v[...], sharp[0]) + dot(inner_v[...], sharp[1])

    pl.semaphore_wait(far_sem.at[1], len(diagonals))
    for dx in (-4, 4):
        pl.semaphore_signal(far_sem.at[2], inc=1, device_id=at(dx, 0), device_id_type=MESH)
    for send in sends[2:]:
        send.wait()

    @pl.when(p == 0)
    def _():
        sides[0:SIDE_ROWS, :] = jnp.zeros((SIDE_ROWS, TILE_Y), jnp.bfloat16)
        corner_in[0] = jnp.zeros(corner_in.shape[1:], jnp.bfloat16)

    @pl.when(p == count_x - 1)
    def _():
        sides[SIDE_ROWS : 2 * SIDE_ROWS, :] = jnp.zeros((SIDE_ROWS, TILE_Y), jnp.bfloat16)
        corner_in[1] = jnp.zeros(corner_in.shape[1:], jnp.bfloat16)

    @pl.when(q == 0)
    def _():
        corner_in[:, 0:16, :] = jnp.zeros((2, 16, corner_in.shape[2]), jnp.bfloat16)

    @pl.when(q == count_y - 1)
    def _():
        corner_in[:, 16:32, :] = jnp.zeros((2, 16, corner_in.shape[2]), jnp.bfloat16)

    for side in range(2):
        side_ends[side * SIDE_ROWS : (side + 1) * SIDE_ROWS, :] = put_columns(
            corner_in[side, :, 0:SIDE_ROWS]
        )
    blurred = []
    for g in range(GROUPS):
        low_rows = slice(WINDOW_AT[g], WINDOW_AT[g] + WINDOW)
        high_rows = slice(SIDE_ROWS + WINDOW_AT[g], SIDE_ROWS + WINDOW_AT[g] + WINDOW)
        window = jnp.concatenate(
            [
                jnp.concatenate([side_ends[low_rows, :], sides[low_rows, :]], axis=1),
                jnp.concatenate([side_ends[high_rows, :], sides[high_rows, :]], axis=1),
            ],
            axis=0,
        )
        blurred.append(
            dot(side_v[g, 0], window) + dot(side_v[g, 1], window) + smooth[g, INNER:GROUP_ROWS, :]
        )
    high, low = indicator(jnp.concatenate(blurred, axis=0))
    low_out = jnp.where(p == 0, 1.0, 0.0)
    high_out = jnp.where(p == count_x - 1, 1.0, 0.0)
    keep = (1.0 - low_out * marks[0:1, :] - high_out * marks[1:2, :]).astype(jnp.bfloat16)
    weights = outer_v[...] * keep
    cells = cells + dot(weights, high) + dot(weights, low)

    high, low = split(cells)
    plain = dot(high[0:96], cell_y_v[0]) + dot(low[0:96], cell_y_v[0])
    slopes = dot(high[96:192], cell_y_v[1]) + dot(low[96:192], cell_y_v[1])
    mean_z, mean_x, mean_y = slopes[0:32, 0:128], slopes[32:64, 0:128], slopes[64:96, 128:256]
    shrink = -lax.rsqrt(mean_z * mean_z + mean_x * mean_x + mean_y * mean_y + normal_floor)
    found = [
        plain[0:32, 0:128],
        plain[32:64, 0:128],
        plain[64:96, 0:128],
        plain[0:32, 128:256],
        mean_z * shrink,
        mean_x * shrink,
        mean_y * shrink,
    ]
    for channel in range(CHANNELS):
        geometry[channel] = found[channel]
    write = pltpu.make_async_copy(geometry, geometry_h, geometry_sem)
    write.start()

    most = functools.reduce(jnp.maximum, [jnp.abs(value) for value in found])
    most = jnp.maximum(jnp.max(most, axis=1, keepdims=True), 1e-37)
    grade = jnp.ceil(8.0 * jnp.log2(most) + 0.02)
    stretch = jnp.exp2(grade * -0.125)
    whole = [jnp.floor(value * stretch * LEVELS + 0.5) for value in found]
    whole.append(jnp.broadcast_to(grade, (ROWS, 128)))
    coded = jnp.concatenate(
        [jnp.concatenate(whole[0:4], axis=0), jnp.concatenate(whole[4:8], axis=0)], axis=1
    )
    upper = jnp.floor(coded * (1.0 / 256.0) + 0.5) * 256.0
    stacked = jnp.concatenate([upper, coded - upper], axis=0).astype(jnp.bfloat16)
    placed = dot(chosen[...], stacked).astype(jnp.int32)
    joined = (placed[:, 128:256] << 16) | (placed[:, 0:128] & 0xFFFF)
    leaving[...] = joined.reshape(count, 8, 128)

    pl.semaphore_wait(far_sem.at[2], 2)

    def send_out(step, carry):
        other = lax.rem(me + step, count)
        pltpu.make_async_remote_copy(
            src_ref=leaving.at[other],
            dst_ref=arrived.at[me],
            send_sem=out_send,
            recv_sem=out_recv,
            device_id=(other // count_y, lax.rem(other, count_y)),
            device_id_type=MESH,
        ).start()
        return carry

    lax.fori_loop(1, count, send_out, 0)
    stay = pltpu.make_async_copy(leaving.at[me], arrived.at[me], own_sem)
    stay.start()
    others = pl.ds(0, count - 1)
    every = pltpu.make_async_remote_copy(
        src_ref=leaving.at[others],
        dst_ref=arrived.at[others],
        send_sem=out_send,
        recv_sem=out_recv,
        device_id=at(1, 0),
        device_id_type=MESH,
    )
    every.wait_send()
    every.wait_recv()
    stay.wait()
    write.wait()


def decode_kernel(
    coded, geometry_in, received, geometry, received_v, copy_sem, store_sem
):
    pieces = store_sem.shape[0]
    rows = received_v.shape[1] // pieces
    whole = pltpu.make_async_copy(geometry_in, geometry, copy_sem)
    whole.start()
    stores = []
    for i in range(pieces):
        target = pl.ds(i * rows, rows)
        stores.append(
            pltpu.make_async_copy(
                received_v.at[:, target, :], received.at[:, target, :], store_sem.at[i]
            )
        )
    for i in range(pieces):
        target = slice(i * rows, (i + 1) * rows)

        def pair(part):
            both = coded[pl.ds(i * rows * 4 + part, rows, stride=4), :]
            return (both << 16) >> 16, both >> 16

        fourth, grade = pair(3)
        scale = jnp.exp2(grade.astype(jnp.float32) * 0.125) * (1.0 / LEVELS)
        received_v[3, target] = fourth.astype(jnp.float32) * scale
        for part in range(3):
            low, high = pair(part)
            received_v[part, target] = low.astype(jnp.float32) * scale
            received_v[part + 4, target] = high.astype(jnp.float32) * scale
        stores[i].start()
    for store in stores:
        store.wait()
    whole.wait()


def body(count_x, count_y, volume, owner, flags):
    count = count_x * count_y
    inner_w, outer_w = cell_matrices()
    take_w, put_w = column_matrices()
    weights = [
        take_w, pack_matrix(), own_matrix(), along_y_matrix(), put_w, inner_w, side_matrices(), outer_w, cell_y_matrix(),
    ]
    anywhere = pl.BlockSpec(memory_space=pl.ANY)
    bf16 = jnp.bfloat16
    marks = side_marks()
    operands = [volume, owner.reshape(1, ROWS), flags.reshape(1, ROWS), marks, *weights]
    operands = [jnp.asarray(value) for value in operands]
    in_vmem = pl.BlockSpec(memory_space=pltpu.VMEM)
    geometry, arrived = pl.pallas_call(
        functools.partial(kernel, count_x, count_y),
        out_shape=(
            pltpu.VMEM((CHANNELS, ROWS, 128), jnp.float32),
            pltpu.VMEM((count, 8, 128), jnp.int32),
        ),
        in_specs=[anywhere] * (4 + len(weights)),
        out_specs=(anywhere, anywhere),
        scratch_shapes=[
            pltpu.VMEM((PLANES_IN, TILE_X, TILE_Y), bf16),
            pltpu.VMEM((2 * SIDE_ROWS, TILE_Y), bf16),
            pltpu.VMEM((32, 896), bf16),
            pltpu.VMEM((2, 32, 256), bf16),
            pltpu.VMEM((2 * SIDE_ROWS, TILE_Y), bf16),
            pltpu.VMEM((32, 896), bf16),
            pltpu.VMEM((2, 32, 256), bf16),
            pltpu.VMEM((OWN, 128), bf16),
            pltpu.VMEM((2 * SIDE_ROWS, 128), bf16),
            pltpu.VMEM((GROUPS, GROUP_ROWS, WIDE_Y), jnp.float32),
            pltpu.VMEM((2, GROUPS * INNER, WIDE_Y), bf16),
            pltpu.VMEM((count * 8, 256), bf16),
            pltpu.VMEM((count, 8, 128), jnp.int32),
            pltpu.VMEM((CHANNELS, ROWS, 128), jnp.float32),
            pltpu.VMEM((1, ROWS), jnp.int32),
            pltpu.VMEM((1, ROWS), jnp.int32),
            pltpu.VMEM(marks.shape, jnp.float32),
            pltpu.VMEM((2, 512, 256), bf16),
        ]
        + [pltpu.VMEM(weight.shape, bf16) for weight in weights if weight is not weights[3]]
        + [
            pltpu.SemaphoreType.DMA((4 + len(weights),)),
            pltpu.SemaphoreType.DMA((8,)),
            pltpu.SemaphoreType.DMA((8,)),
            pltpu.SemaphoreType.REGULAR((3,)),
            pltpu.SemaphoreType.DMA,
            pltpu.SemaphoreType.DMA,
            pltpu.SemaphoreType.DMA,
            pltpu.SemaphoreType.DMA,
        ],
        compiler_params=pltpu.CompilerParams(
            collective_id=0, has_side_effects=True, vmem_limit_bytes=40 * 2**20
        ),
    )(*[pltpu.with_memory_space_constraint(value, pltpu.HBM) for value in operands])
    pieces = 4
    received, geometry = pl.pallas_call(
        decode_kernel,
        out_shape=(
            jax.ShapeDtypeStruct((CHANNELS, count * 2, 128), jnp.float32),
            jax.ShapeDtypeStruct(geometry.shape, jnp.float32),
        ),
        in_specs=[in_vmem, in_vmem],
        out_specs=(anywhere, anywhere),
        scratch_shapes=[
            pltpu.VMEM((CHANNELS, count * 2, 128), jnp.float32),
            pltpu.SemaphoreType.DMA,
            pltpu.SemaphoreType.DMA((pieces,)),
        ],
        compiler_params=pltpu.CompilerParams(vmem_limit_bytes=16 * 2**20),
    )(arrived.reshape(count * 8, 128), geometry)
    received = jnp.transpose(received, (1, 0, 2))[None]
    return (geometry.reshape(CHANNELS, 4, 8, 128), received)


def solution(mesh):
    in_specs = (P(None, "gx", "gy"), P("gx", "gy", None, None), P("gx", "gy", None))
    out_specs = (P(None, None, "gx", "gy"), P(("gx", "gy"), None, None, None))
    return jax.shard_map(
        functools.partial(body, mesh.shape["gx"], mesh.shape["gy"]),
        mesh=mesh,
        in_specs=in_specs,
        out_specs=out_specs,
        check_vma=False,
    )
```

```python
import functools
import math

import jax
import jax.numpy as jnp
import ml_dtypes
import numpy as np
from jax import lax
from jax.experimental import pallas as pl
from jax.experimental.pallas import tpu as pltpu
from jax.sharding import PartitionSpec as P

MESH = pl.DeviceIdType.MESH

raw_taps = [math.exp(-((offset - 4) ** 2) / 8.0) for offset in range(9)]
gauss_taps = np.array([value / sum(raw_taps) for value in raw_taps])
sharpness = 20.0
normal_floor = 0.01

PLANES_IN = 26
TILE_X = 32
TILE_Y = 512
OWN = PLANES_IN * TILE_X
REACH = 5
WIDE_X = TILE_X + 2
GROUPS = 3
GROUP_PLANES = 6
GROUP_IN = GROUP_PLANES + 8
INNER_X = 24
OUTER_X = 10
INNER = GROUP_PLANES * INNER_X
OUTER = 64
GROUP_ROWS = INNER + OUTER
SIDE_ROWS = 144
WINDOW = 96
WINDOW_AT = [(REACH * GROUP_PLANES * g) // 16 * 16 for g in range(GROUPS)]
PACK_PLANES = 8
PACK_ROWS = PACK_PLANES * REACH
WIDE_Y = TILE_Y + 128
BAND = (112, 400)
ROWS = 32
CHANNELS = 7
LEVELS = 32766.0


def outer_place(x):
    if x < REACH:
        return x
    return x - INNER_X if x >= REACH + INNER_X else None


def row_of(plane, x):
    outer = outer_place(x)
    if outer is None:
        return plane * INNER_X + x - REACH
    return INNER + plane * OUTER_X + outer


def halves(matrix):
    high = matrix.astype(np.float32).astype(ml_dtypes.bfloat16)
    low = (matrix - high.astype(np.float64)).astype(np.float32).astype(ml_dtypes.bfloat16)
    return np.stack([high, low])


def pack_matrix():
    matrix = np.zeros((2 * PACK_ROWS, PACK_PLANES * TILE_X))
    for z in range(PACK_PLANES):
        for i in range(REACH):
            matrix[z * REACH + i, z * TILE_X + i] = 1
            matrix[PACK_ROWS + z * REACH + i, z * TILE_X + TILE_X - REACH + i] = 1
    return matrix.astype(ml_dtypes.bfloat16)


def column_matrices():
    take = np.zeros((32, 256))
    put = np.zeros((32, 128))
    for i in range(REACH):
        take[i, i] = 1
        take[16 + i, 256 - REACH + i] = 1
        put[i, 128 - REACH + i] = 1
        put[16 + i, i] = 1
    return take.astype(ml_dtypes.bfloat16), put.astype(ml_dtypes.bfloat16)


def tap(distance):
    return gauss_taps[distance + 4] if -4 <= distance <= 4 else 0.0


def own_matrix():
    matrix = np.zeros((GROUP_ROWS, GROUP_IN * TILE_X))
    for plane in range(GROUP_PLANES):
        for x in range(WIDE_X):
            for z in range(9):
                for source in range(TILE_X):
                    matrix[row_of(plane, x), (plane + z) * TILE_X + source] = (
                        gauss_taps[z] * tap(source - (x - 1))
                    )
    return halves(matrix)


def side_matrices():
    found = []
    for g in range(GROUPS):
        matrix = np.zeros((OUTER, 2 * WINDOW))
        for plane in range(GROUP_PLANES):
            for x in range(WIDE_X):
                outer = outer_place(x)
                if outer is None:
                    continue
                for z in range(9):
                    for i in range(REACH):
                        row = (g * GROUP_PLANES + plane + z) * REACH + i - WINDOW_AT[g]
                        out = plane * OUTER_X + outer
                        matrix[out, row] = gauss_taps[z] * tap(i - REACH - (x - 1))
                        matrix[out, WINDOW + row] = gauss_taps[z] * tap(TILE_X + i - (x - 1))
        found.append(halves(matrix))
    return np.stack(found)


def along_y_matrix():
    scale = -sharpness / math.log(2.0)
    main = np.zeros((512, 256))
    for out in range(256):
        for distance in range(-4, 5):
            main[128 + out + distance, out] = scale * tap(distance)
    return halves(main)[:, BAND[0] : BAND[1]]


MEAN = np.array([0, 1, 1, 1, 1, 0]) / 4
FIRST = np.array([0, 1, 0, 0, 0, 0]) / 1
SOFT = np.array([1, 3, 4, 4, 3, 1]) / 16
SLOPE = np.array([-1, -1, 0, 0, 1, 1]) / 8


def cell_matrices():
    pairs = [(MEAN, MEAN), (FIRST, MEAN), (MEAN, FIRST), (SLOPE, SOFT), (SOFT, SLOPE), (SOFT, SOFT)]
    inner = np.zeros((len(pairs) * ROWS, GROUPS * INNER))
    outer = np.zeros((len(pairs) * ROWS, GROUPS * OUTER))
    for at, (along_z, along_x) in enumerate(pairs):
        for layer in range(4):
            for cell in range(8):
                for z in range(6):
                    for x in range(6):
                        group, plane = divmod(4 * layer + z, GROUP_PLANES)
                        row = row_of(plane, 4 * cell + x)
                        out = at * ROWS + layer * 8 + cell
                        weight = along_z[z] * along_x[x]
                        if row < INNER:
                            inner[out, group * INNER + row] += weight
                        else:
                            outer[out, group * OUTER + row - INNER] += weight
    return inner.astype(ml_dtypes.bfloat16), outer.astype(ml_dtypes.bfloat16)


def cell_y_matrix():
    matrix = np.zeros((2, TILE_Y + 128, 256))
    for at, weights in enumerate((MEAN, FIRST, SOFT, SLOPE)):
        for cell in range(128):
            for y in range(6):
                place = 4 * cell + y - 1
                row = TILE_Y + 127 if place < 0 else place
                matrix[at // 2, row, at % 2 * 128 + cell] = weights[y]
    return matrix.astype(ml_dtypes.bfloat16)


def side_marks():
    marks = np.zeros((8, GROUPS * OUTER), np.float32)
    for group in range(GROUPS):
        for plane in range(GROUP_PLANES):
            marks[0, group * OUTER + plane * OUTER_X] = 1
            marks[1, group * OUTER + plane * OUTER_X + OUTER_X - 1] = 1
    return marks


def split(value):
    high = value.astype(jnp.bfloat16)
    return high, (value - high.astype(jnp.float32)).astype(jnp.bfloat16)


def dot(left, right):
    return jnp.dot(left, right, preferred_element_type=jnp.float32)


def routing(owner, flags):
    wide = (ROWS, ROWS)
    row = lax.broadcasted_iota(jnp.int32, wide, 0)
    column = lax.broadcasted_iota(jnp.int32, wide, 1)
    owner_across = jnp.broadcast_to(owner.astype(jnp.float32), wide)
    flag_across = jnp.broadcast_to(flags.astype(jnp.float32), wide)
    same = row == column
    owner_down = jnp.sum(jnp.where(same, owner_across, 0.0), axis=1, keepdims=True)
    flag_down = jnp.sum(jnp.where(same, flag_across, 0.0), axis=1, keepdims=True)
    earlier = (column < row) & (owner_down == owner_across)
    slot = jnp.sum(jnp.where(earlier, flag_across, 0.0), axis=1, keepdims=True)
    code = jnp.where(flag_down > 0.5, owner_down * 2.0 + slot, -8.0)
    place = lax.broadcasted_iota(jnp.int32, (ROWS, 256), 1)
    mine = (place & (ROWS - 1)) == lax.broadcasted_iota(jnp.int32, (ROWS, 256), 0)
    spread = jnp.sum(jnp.where(mine, code, 0.0), axis=0, keepdims=True)
    part = ((lax.broadcasted_iota(jnp.int32, (1, 256), 1) >> 5) & 3).astype(jnp.float32)
    return spread * 4.0 + part


def kernel(
    count_x, count_y,
    volume, owner_h, flags_h, marks_h,
    take_w, pack_w, own_w, main_w, put_w, inner_w, side_w, outer_w, cell_y_w,
    geometry_h, arrived,
    tile, packed, columns, corners, sides, beside, corner_in, ends, side_ends,
    smooth, sharp, chosen, stacked, leaving, geometry, owner, flags, marks, main_v,
    take_v, pack_v, own_v, put_v, inner_v, side_v, outer_v, cell_y_v,
    load_sem, send_sem, recv_sem, far_sem, out_send, out_recv, own_sem, geometry_sem,
):
    p = lax.axis_index("gx")
    q = lax.axis_index("gy")
    count = count_x * count_y
    me = p * count_y + q

    def at(dx, dy):
        return (lax.rem(p + dx + count_x, count_x), lax.rem(q + dy + count_y, count_y))

    around = [(0, -1), (0, 1), (-1, 0), (1, 0), (-1, -1), (-1, 1), (1, -1), (1, 1)]
    barrier = pltpu.get_barrier_semaphore()
    for dx, dy in around:
        pl.semaphore_signal(barrier, inc=1, device_id=at(dx, dy), device_id_type=MESH)
    pairs = [
        (volume, tile),
        (pack_w, pack_v),
        (take_w, take_v),
        (own_w, own_v),
        (owner_h, owner),
        (flags_h, flags),
        (put_w, put_v),
        (main_w, main_v.at[:, pl.ds(BAND[0], BAND[1] - BAND[0]), :]),
        (inner_w, inner_v),
        (side_w, side_v),
        (marks_h, marks),
        (outer_w, outer_v),
        (cell_y_w, cell_y_v),
    ]
    loads = [pltpu.make_async_copy(*pair, load_sem.at[i]) for i, pair in enumerate(pairs)]
    for load in loads[0:4]:
        load.start()
    main_v[:, 0 : BAND[0], :] = jnp.zeros((2, BAND[0], 256), jnp.bfloat16)
    main_v[:, BAND[1] : 512, :] = jnp.zeros((2, 512 - BAND[1], 256), jnp.bfloat16)

    def take_columns(rows):
        both = jnp.concatenate([rows[:, 0:128], rows[:, TILE_Y - 128 : TILE_Y]], axis=1)
        return lax.dot_general(
            take_v[...], both, (((1,), (1,)), ((), ())), preferred_element_type=jnp.float32
        ).astype(jnp.bfloat16)

    def put_columns(taken):
        left_keep = jnp.where(q == 0, 0.0, 1.0)
        right_keep = jnp.where(q == count_y - 1, 0.0, 1.0)
        line = lax.broadcasted_iota(jnp.int32, (32, 128), 0)
        inside = jnp.where(line < 16, left_keep, right_keep).astype(jnp.bfloat16)
        return lax.dot_general(
            taken, put_v[...] * inside, (((0,), (0,)), ((), ())), preferred_element_type=jnp.float32
        ).astype(jnp.bfloat16)

    for load in loads[0:3]:
        load.wait()
    for load in loads[4:]:
        load.start()
    own = tile[...].reshape(OWN, TILE_Y)
    low_rows, high_rows = [], []
    for first in range(0, PLANES_IN, PACK_PLANES):
        block = own[first * TILE_X : min(first + PACK_PLANES, PLANES_IN) * TILE_X]
        taken = dot(pack_v[:, 0 : block.shape[0]], block)
        rows = min(PACK_ROWS, SIDE_ROWS - first * REACH)
        low_rows.append(taken[0:rows])
        high_rows.append(taken[PACK_ROWS : PACK_ROWS + rows])
    edge_rows = jnp.concatenate(low_rows + high_rows, axis=0).astype(jnp.bfloat16)
    packed[...] = edge_rows
    columns[:, 0:OWN] = take_columns(own)
    for side in range(2):
        corners[side, :, 0:SIDE_ROWS] = take_columns(
            edge_rows[side * SIDE_ROWS : (side + 1) * SIDE_ROWS]
        )

    pl.semaphore_wait(barrier, len(around))
    diagonals = around[4:]
    for dx, dy in diagonals:
        pl.semaphore_signal(far_sem.at[0], inc=1, device_id=at(dx, dy), device_id_type=MESH)
    sends = []
    for i, (dx, dy) in enumerate(around):
        rows, rows_there = (0, SIDE_ROWS) if dx < 0 else (SIDE_ROWS, 0)
        lines, lines_there = (0, 16) if dy < 0 else (16, 0)
        if dx == 0:
            source = columns.at[pl.ds(lines, 16), :]
            target = beside.at[pl.ds(lines_there, 16), :]
        elif dy == 0:
            source = packed.at[pl.ds(rows, SIDE_ROWS), :]
            target = sides.at[pl.ds(rows_there, SIDE_ROWS), :]
        else:
            source = corners.at[rows // SIDE_ROWS, pl.ds(lines, 16), :]
            target = corner_in.at[rows_there // SIDE_ROWS, pl.ds(lines_there, 16), :]
        sends.append(
            pltpu.make_async_remote_copy(
                src_ref=source,
                dst_ref=target,
                send_sem=send_sem.at[i],
                recv_sem=recv_sem.at[i],
                device_id=at(dx, dy),
                device_id_type=MESH,
            )
        )
    for send in sends:
        send.start()

    loads[3].wait()
    for g in range(GROUPS):
        block = tile[g * GROUP_PLANES : g * GROUP_PLANES + GROUP_IN].reshape(
            GROUP_IN * TILE_X, TILE_Y
        )
        smooth[g, :, 128:WIDE_Y] = dot(own_v[0], block) + dot(own_v[1], block)

    for load in loads[4:6]:
        load.wait()
    codes = routing(owner[...], flags[...])
    number = lax.broadcasted_iota(jnp.int32, (count * 8, 256), 0).astype(jnp.float32)
    chosen[...] = jnp.where(number == codes, 1.0, 0.0).astype(jnp.bfloat16)

    pl.semaphore_wait(far_sem.at[0], len(diagonals))
    for dx, dy in diagonals:
        pl.semaphore_signal(
            far_sem.at[1], inc=1, device_id=at(2 * dx, 2 * dy), device_id_type=MESH
        )
    for load in loads[6:]:
        load.wait()
    for send in sends[0:2]:
        send.wait()

    lane = lax.broadcasted_iota(jnp.int32, (1, 128), 1)
    left_out = jnp.where(q == 0, 127, -1)
    right_out = jnp.where(q == count_y - 1, 0, -1)
    edge_keep = jnp.where((lane == left_out) | (lane == right_out), 0.0, 1.0)

    def sigmoid_of(power):
        below = 1.0 + jnp.exp2(jnp.minimum(power, 126.0))
        guess = pl.reciprocal(below, approx=True)
        return guess * (2.0 - below * guess)

    def indicator(blurred):
        high, low = split(blurred)

        def along_y(choose, weights):
            high_part = choose(high)
            return (
                dot(high_part, weights[0])
                + dot(choose(low), weights[0])
                + dot(high_part, weights[1])
            )

        def last(part):
            return jnp.concatenate([part[:, 256:WIDE_Y], part[:, 0:128]], axis=1)

        def right_end(part):
            return jnp.concatenate([part[:, 512:WIDE_Y], part[:, 0:128]], axis=1)

        left = along_y(lambda part: part[:, 0:256], main_v[:, 128:384, 0:128])
        right = along_y(right_end, main_v[:, 128:384, 128:256])
        edge = jnp.where(lane == 127, left, right)
        return split(
            jnp.concatenate(
                [
                    sigmoid_of(along_y(lambda part: part[:, 0:512], main_v[...])),
                    sigmoid_of(along_y(last, main_v[...])),
                    edge_keep * sigmoid_of(edge),
                ],
                axis=1,
            )
        )

    ends[...] = put_columns(beside[:, 0:OWN])
    for g in range(GROUPS):
        first = g * GROUP_PLANES * TILE_X
        block = ends[first : first + GROUP_IN * TILE_X, :]
        smooth[g, :, 0:128] = dot(own_v[0], block) + dot(own_v[1], block)
        high, low = indicator(smooth[g, 0:INNER, :])
        sharp[0, g * INNER : (g + 1) * INNER, :] = high
        sharp[1, g * INNER : (g + 1) * INNER, :] = low
    cells = dot(inner_v[...], sharp[0]) + dot(inner_v[...], sharp[1])

    pl.semaphore_wait(far_sem.at[1], len(diagonals))
    for dx in (-4, 4):
        pl.semaphore_signal(far_sem.at[2], inc=1, device_id=at(dx, 0), device_id_type=MESH)
    for send in sends[2:]:
        send.wait()

    for side in range(2):
        side_ends[side * SIDE_ROWS : (side + 1) * SIDE_ROWS, :] = put_columns(
            corner_in[side, :, 0:SIDE_ROWS]
        )
    low_out = jnp.where(p == 0, 1.0, 0.0)
    high_out = jnp.where(p == count_x - 1, 1.0, 0.0)
    place = lax.broadcasted_iota(jnp.int32, (1, 2 * WINDOW), 1)
    side_keep = jnp.where(place < WINDOW, 1.0 - low_out, 1.0 - high_out).astype(jnp.bfloat16)
    blurred = []
    for g in range(GROUPS):
        low_rows = slice(WINDOW_AT[g], WINDOW_AT[g] + WINDOW)
        high_rows = slice(SIDE_ROWS + WINDOW_AT[g], SIDE_ROWS + WINDOW_AT[g] + WINDOW)
        window = jnp.concatenate(
            [
                jnp.concatenate([side_ends[low_rows, :], sides[low_rows, :]], axis=1),
                jnp.concatenate([side_ends[high_rows, :], sides[high_rows, :]], axis=1),
            ],
            axis=0,
        )
        blurred.append(
            dot(side_v[g, 0] * side_keep, window)
            + dot(side_v[g, 1] * side_keep, window)
            + smooth[g, INNER:GROUP_ROWS, :]
        )
    high, low = indicator(jnp.concatenate(blurred, axis=0))
    keep = (1.0 - low_out * marks[0:1, :] - high_out * marks[1:2, :]).astype(jnp.bfloat16)
    weights = outer_v[...] * keep
    cells = cells + dot(weights, high) + dot(weights, low)

    high, low = split(cells)
    plain = dot(high[0:96], cell_y_v[0]) + dot(low[0:96], cell_y_v[0])
    slopes = dot(high[96:192], cell_y_v[1]) + dot(low[96:192], cell_y_v[1])
    mean_z, mean_x, mean_y = slopes[0:32, 0:128], slopes[32:64, 0:128], slopes[64:96, 128:256]
    shrink = -lax.rsqrt(mean_z * mean_z + mean_x * mean_x + mean_y * mean_y + normal_floor)
    found = [
        plain[0:32, 0:128],
        plain[32:64, 0:128],
        plain[64:96, 0:128],
        plain[0:32, 128:256],
        mean_z * shrink,
        mean_x * shrink,
        mean_y * shrink,
    ]
    for channel in range(CHANNELS):
        geometry[channel] = found[channel]
    write = pltpu.make_async_copy(geometry, geometry_h, geometry_sem)
    write.start()

    most = functools.reduce(jnp.maximum, [jnp.abs(value) for value in found])
    most = jnp.maximum(jnp.max(most, axis=1, keepdims=True), 1e-37)
    grade = jnp.ceil(8.0 * jnp.log2(most) + 0.02)
    stretch = jnp.exp2(grade * -0.125)
    whole = [jnp.floor(value * stretch * LEVELS + 0.5) for value in found]
    whole.append(jnp.broadcast_to(grade, (ROWS, 128)))
    coded = jnp.concatenate(
        [jnp.concatenate(whole[0:4], axis=0), jnp.concatenate(whole[4:8], axis=0)], axis=1
    )
    upper = jnp.floor(coded * (1.0 / 256.0) + 0.5) * 256.0
    stacked[...] = jnp.concatenate([upper, coded - upper], axis=0).astype(jnp.bfloat16)

    def send_to_row(offset, first_step):
        other_p = lax.rem(p + offset, count_x)
        rows = pl.ds(pl.multiple_of(other_p * (count_y * 8), count_y * 8), count_y * 8)
        placed = dot(chosen[rows, :], stacked[...]).astype(jnp.int32)
        joined = (placed[:, 128:256] << 16) | (placed[:, 0:128] & 0xFFFF)
        leaving[pl.ds(other_p * count_y, count_y)] = joined.reshape(count_y, 8, 128)
        for step in range(first_step, count_y):
            other_q = lax.rem(q + step, count_y)
            pltpu.make_async_remote_copy(
                src_ref=leaving.at[other_p * count_y + other_q],
                dst_ref=arrived.at[me],
                send_sem=out_send,
                recv_sem=out_recv,
                device_id=(other_p, other_q),
                device_id_type=MESH,
            ).start()

    def send_rows(offset, carry):
        send_to_row(offset, 0)
        return carry

    send_to_row(0, 1)
    lax.fori_loop(1, 5, send_rows, 0)
    lax.fori_loop(count_x - 4, count_x, send_rows, 0)
    pl.semaphore_wait(far_sem.at[2], 2)
    lax.fori_loop(5, count_x - 4, send_rows, 0)
    stay = pltpu.make_async_copy(leaving.at[me], arrived.at[me], own_sem)
    stay.start()
    others = pl.ds(0, count - 1)
    every = pltpu.make_async_remote_copy(
        src_ref=leaving.at[others],
        dst_ref=arrived.at[others],
        send_sem=out_send,
        recv_sem=out_recv,
        device_id=at(1, 0),
        device_id_type=MESH,
    )
    every.wait_send()
    every.wait_recv()
    stay.wait()
    write.wait()


def decode_kernel(
    coded, geometry_in, received, geometry, received_v, copy_sem, store_sem
):
    pieces = store_sem.shape[0]
    rows = received_v.shape[1] // pieces
    whole = pltpu.make_async_copy(geometry_in, geometry, copy_sem)
    whole.start()
    stores = []
    for i in range(pieces):
        target = pl.ds(i * rows, rows)
        stores.append(
            pltpu.make_async_copy(
                received_v.at[:, target, :], received.at[:, target, :], store_sem.at[i]
            )
        )
    for i in range(pieces):
        target = slice(i * rows, (i + 1) * rows)

        def pair(part):
            both = coded[pl.ds(i * rows * 4 + part, rows, stride=4), :]
            return (both << 16) >> 16, both >> 16

        fourth, grade = pair(3)
        scale = jnp.exp2(grade.astype(jnp.float32) * 0.125) * (1.0 / LEVELS)
        received_v[3, target] = fourth.astype(jnp.float32) * scale
        for part in range(3):
            low, high = pair(part)
            received_v[part, target] = low.astype(jnp.float32) * scale
            received_v[part + 4, target] = high.astype(jnp.float32) * scale
        stores[i].start()
    for store in stores:
        store.wait()
    whole.wait()


def body(count_x, count_y, volume, owner, flags):
    count = count_x * count_y
    inner_w, outer_w = cell_matrices()
    take_w, put_w = column_matrices()
    weights = [
        take_w, pack_matrix(), own_matrix(), along_y_matrix(), put_w, inner_w, side_matrices(), outer_w, cell_y_matrix(),
    ]
    anywhere = pl.BlockSpec(memory_space=pl.ANY)
    bf16 = jnp.bfloat16
    marks = side_marks()
    operands = [volume, owner.reshape(1, ROWS), flags.reshape(1, ROWS), marks, *weights]
    operands = [jnp.asarray(value) for value in operands]
    in_vmem = pl.BlockSpec(memory_space=pltpu.VMEM)
    geometry, arrived = pl.pallas_call(
        functools.partial(kernel, count_x, count_y),
        out_shape=(
            pltpu.VMEM((CHANNELS, ROWS, 128), jnp.float32),
            pltpu.VMEM((count, 8, 128), jnp.int32),
        ),
        in_specs=[anywhere] * (4 + len(weights)),
        out_specs=(anywhere, anywhere),
        scratch_shapes=[
            pltpu.VMEM((PLANES_IN, TILE_X, TILE_Y), bf16),
            pltpu.VMEM((2 * SIDE_ROWS, TILE_Y), bf16),
            pltpu.VMEM((32, 896), bf16),
            pltpu.VMEM((2, 32, 256), bf16),
            pltpu.VMEM((2 * SIDE_ROWS, TILE_Y), bf16),
            pltpu.VMEM((32, 896), bf16),
            pltpu.VMEM((2, 32, 256), bf16),
            pltpu.VMEM((OWN, 128), bf16),
            pltpu.VMEM((2 * SIDE_ROWS, 128), bf16),
            pltpu.VMEM((GROUPS, GROUP_ROWS, WIDE_Y), jnp.float32),
            pltpu.VMEM((2, GROUPS * INNER, WIDE_Y), bf16),
            pltpu.VMEM((count * 8, 256), bf16),
            pltpu.VMEM((256, 256), bf16),
            pltpu.VMEM((count, 8, 128), jnp.int32),
            pltpu.VMEM((CHANNELS, ROWS, 128), jnp.float32),
            pltpu.VMEM((1, ROWS), jnp.int32),
            pltpu.VMEM((1, ROWS), jnp.int32),
            pltpu.VMEM(marks.shape, jnp.float32),
            pltpu.VMEM((2, 512, 256), bf16),
        ]
        + [pltpu.VMEM(weight.shape, bf16) for weight in weights if weight is not weights[3]]
        + [
            pltpu.SemaphoreType.DMA((4 + len(weights),)),
            pltpu.SemaphoreType.DMA((8,)),
            pltpu.SemaphoreType.DMA((8,)),
            pltpu.SemaphoreType.REGULAR((3,)),
            pltpu.SemaphoreType.DMA,
            pltpu.SemaphoreType.DMA,
            pltpu.SemaphoreType.DMA,
            pltpu.SemaphoreType.DMA,
        ],
        compiler_params=pltpu.CompilerParams(
            collective_id=0, has_side_effects=True, vmem_limit_bytes=40 * 2**20
        ),
    )(*[pltpu.with_memory_space_constraint(value, pltpu.HBM) for value in operands])
    pieces = 4
    received, geometry = pl.pallas_call(
        decode_kernel,
        out_shape=(
            jax.ShapeDtypeStruct((CHANNELS, count * 2, 128), jnp.float32),
            jax.ShapeDtypeStruct(geometry.shape, jnp.float32),
        ),
        in_specs=[in_vmem, in_vmem],
        out_specs=(anywhere, anywhere),
        scratch_shapes=[
            pltpu.VMEM((CHANNELS, count * 2, 128), jnp.float32),
            pltpu.SemaphoreType.DMA,
            pltpu.SemaphoreType.DMA((pieces,)),
        ],
        compiler_params=pltpu.CompilerParams(vmem_limit_bytes=16 * 2**20),
    )(arrived.reshape(count * 8, 128), geometry)
    received = jnp.transpose(received, (1, 0, 2))[None]
    return (geometry.reshape(CHANNELS, 4, 8, 128), received)


def solution(mesh):
    in_specs = (P(None, "gx", "gy"), P("gx", "gy", None, None), P("gx", "gy", None))
    out_specs = (P(None, None, "gx", "gy"), P(("gx", "gy"), None, None, None))
    return jax.shard_map(
        functools.partial(body, mesh.shape["gx"], mesh.shape["gy"]),
        mesh=mesh,
        in_specs=in_specs,
        out_specs=out_specs,
        check_vma=False,
    )
```

```python
import functools
import math

import jax
import jax.numpy as jnp
import ml_dtypes
import numpy as np
from jax import lax
from jax.experimental import pallas as pl
from jax.experimental.pallas import tpu as pltpu
from jax.sharding import PartitionSpec as P

MESH = pl.DeviceIdType.MESH

raw_taps = [math.exp(-((offset - 4) ** 2) / 8.0) for offset in range(9)]
gauss_taps = np.array([value / sum(raw_taps) for value in raw_taps])
sharpness = 20.0
normal_floor = 0.01

PLANES_IN = 26
TILE_X = 32
TILE_Y = 512
OWN = PLANES_IN * TILE_X
REACH = 5
WIDE_X = TILE_X + 2
GROUPS = 3
GROUP_PLANES = 6
GROUP_IN = GROUP_PLANES + 8
INNER_X = 24
OUTER_X = 10
INNER = GROUP_PLANES * INNER_X
OUTER = 64
GROUP_ROWS = INNER + OUTER
SIDE_ROWS = 144
WINDOW = 96
WINDOW_AT = [(REACH * GROUP_PLANES * g) // 16 * 16 for g in range(GROUPS)]
PACK_PLANES = 8
PACK_ROWS = PACK_PLANES * REACH
WIDE_Y = TILE_Y + 128
BAND = (112, 400)
ROWS = 32
CHANNELS = 7
LEVELS = 32766.0


def outer_place(x):
    if x < REACH:
        return x
    return x - INNER_X if x >= REACH + INNER_X else None


def row_of(plane, x):
    outer = outer_place(x)
    if outer is None:
        return plane * INNER_X + x - REACH
    return INNER + plane * OUTER_X + outer


def halves(matrix):
    high = matrix.astype(np.float32).astype(ml_dtypes.bfloat16)
    low = (matrix - high.astype(np.float64)).astype(np.float32).astype(ml_dtypes.bfloat16)
    return np.stack([high, low])


def pack_matrix():
    matrix = np.zeros((2 * PACK_ROWS, PACK_PLANES * TILE_X))
    for z in range(PACK_PLANES):
        for i in range(REACH):
            matrix[z * REACH + i, z * TILE_X + i] = 1
            matrix[PACK_ROWS + z * REACH + i, z * TILE_X + TILE_X - REACH + i] = 1
    return matrix.astype(ml_dtypes.bfloat16)


def column_matrices():
    take = np.zeros((32, 256))
    put = np.zeros((32, 128))
    for i in range(REACH):
        take[i, i] = 1
        take[16 + i, 256 - REACH + i] = 1
        put[i, 128 - REACH + i] = 1
        put[16 + i, i] = 1
    return take.astype(ml_dtypes.bfloat16), put.astype(ml_dtypes.bfloat16)


def tap(distance):
    return gauss_taps[distance + 4] if -4 <= distance <= 4 else 0.0


def own_matrix():
    matrix = np.zeros((GROUP_ROWS, GROUP_IN * TILE_X))
    for plane in range(GROUP_PLANES):
        for x in range(WIDE_X):
            for z in range(9):
                for source in range(TILE_X):
                    matrix[row_of(plane, x), (plane + z) * TILE_X + source] = (
                        gauss_taps[z] * tap(source - (x - 1))
                    )
    return halves(matrix)


def side_matrices():
    found = []
    for g in range(GROUPS):
        matrix = np.zeros((OUTER, 2 * WINDOW))
        for plane in range(GROUP_PLANES):
            for x in range(WIDE_X):
                outer = outer_place(x)
                if outer is None:
                    continue
                for z in range(9):
                    for i in range(REACH):
                        row = (g * GROUP_PLANES + plane + z) * REACH + i - WINDOW_AT[g]
                        out = plane * OUTER_X + outer
                        matrix[out, row] = gauss_taps[z] * tap(i - REACH - (x - 1))
                        matrix[out, WINDOW + row] = gauss_taps[z] * tap(TILE_X + i - (x - 1))
        found.append(halves(matrix))
    return np.stack(found)


def along_y_matrix():
    scale = -sharpness / math.log(2.0)
    main = np.zeros((512, 256))
    for out in range(256):
        for distance in range(-4, 5):
            main[128 + out + distance, out] = scale * tap(distance)
    return halves(main)[:, BAND[0] : BAND[1]]


MEAN = np.array([0, 1, 1, 1, 1, 0]) / 4
FIRST = np.array([0, 1, 0, 0, 0, 0]) / 1
SOFT = np.array([1, 3, 4, 4, 3, 1]) / 16
SLOPE = np.array([-1, -1, 0, 0, 1, 1]) / 8


def cell_matrices():
    pairs = [(MEAN, MEAN), (FIRST, MEAN), (MEAN, FIRST), (SLOPE, SOFT), (SOFT, SLOPE), (SOFT, SOFT)]
    inner = np.zeros((len(pairs) * ROWS, GROUPS * INNER))
    outer = np.zeros((len(pairs) * ROWS, GROUPS * OUTER))
    for at, (along_z, along_x) in enumerate(pairs):
        for layer in range(4):
            for cell in range(8):
                for z in range(6):
                    for x in range(6):
                        group, plane = divmod(4 * layer + z, GROUP_PLANES)
                        row = row_of(plane, 4 * cell + x)
                        out = at * ROWS + layer * 8 + cell
                        weight = along_z[z] * along_x[x]
                        if row < INNER:
                            inner[out, group * INNER + row] += weight
                        else:
                            outer[out, group * OUTER + row - INNER] += weight
    return inner.astype(ml_dtypes.bfloat16), outer.astype(ml_dtypes.bfloat16)


def cell_y_matrix():
    matrix = np.zeros((2, TILE_Y + 128, 256))
    for at, weights in enumerate((MEAN, FIRST, SOFT, SLOPE)):
        for cell in range(128):
            for y in range(6):
                place = 4 * cell + y - 1
                row = TILE_Y + 127 if place < 0 else place
                matrix[at // 2, row, at % 2 * 128 + cell] = weights[y]
    return matrix.astype(ml_dtypes.bfloat16)


def side_marks():
    marks = np.zeros((8, GROUPS * OUTER), np.float32)
    for group in range(GROUPS):
        for plane in range(GROUP_PLANES):
            marks[0, group * OUTER + plane * OUTER_X] = 1
            marks[1, group * OUTER + plane * OUTER_X + OUTER_X - 1] = 1
    return marks


def split(value):
    high = value.astype(jnp.bfloat16)
    return high, (value - high.astype(jnp.float32)).astype(jnp.bfloat16)


def dot(left, right):
    return jnp.dot(left, right, preferred_element_type=jnp.float32)


def routing(owner, flags):
    wide = (ROWS, ROWS)
    row = lax.broadcasted_iota(jnp.int32, wide, 0)
    column = lax.broadcasted_iota(jnp.int32, wide, 1)
    owner_across = jnp.broadcast_to(owner.astype(jnp.float32), wide)
    flag_across = jnp.broadcast_to(flags.astype(jnp.float32), wide)
    same = row == column
    owner_down = jnp.sum(jnp.where(same, owner_across, 0.0), axis=1, keepdims=True)
    flag_down = jnp.sum(jnp.where(same, flag_across, 0.0), axis=1, keepdims=True)
    earlier = (column < row) & (owner_down == owner_across)
    slot = jnp.sum(jnp.where(earlier, flag_across, 0.0), axis=1, keepdims=True)
    code = jnp.where(flag_down > 0.5, owner_down * 2.0 + slot, -8.0)
    place = lax.broadcasted_iota(jnp.int32, (ROWS, 256), 1)
    mine = (place & (ROWS - 1)) == lax.broadcasted_iota(jnp.int32, (ROWS, 256), 0)
    spread = jnp.sum(jnp.where(mine, code, 0.0), axis=0, keepdims=True)
    part = ((lax.broadcasted_iota(jnp.int32, (1, 256), 1) >> 5) & 3).astype(jnp.float32)
    return spread * 4.0 + part


def kernel(
    count_x, count_y,
    volume, owner_h, flags_h, marks_h,
    take_w, pack_w, own_w, main_w, put_w, inner_w, side_w, outer_w, cell_y_w,
    geometry_h, arrived,
    tile, packed, columns, corners, sides, beside, corner_in, ends, side_ends,
    smooth, sharp, chosen, stacked, leaving, geometry, owner, flags, marks, main_v,
    take_v, pack_v, own_v, put_v, inner_v, side_v, outer_v, cell_y_v,
    load_sem, send_sem, recv_sem, far_sem, out_send, out_recv, own_sem, geometry_sem,
):
    p = lax.axis_index("gx")
    q = lax.axis_index("gy")
    count = count_x * count_y
    me = p * count_y + q

    def at(dx, dy):
        return (lax.rem(p + dx + count_x, count_x), lax.rem(q + dy + count_y, count_y))

    around = [(0, -1), (0, 1), (-1, 0), (1, 0), (-1, -1), (-1, 1), (1, -1), (1, 1)]
    barrier = pltpu.get_barrier_semaphore()
    for dx, dy in around:
        pl.semaphore_signal(barrier, inc=1, device_id=at(dx, dy), device_id_type=MESH)
    pairs = [
        (volume, tile),
        (pack_w, pack_v),
        (take_w, take_v),
        (own_w, own_v),
        (owner_h, owner),
        (flags_h, flags),
        (put_w, put_v),
        (main_w, main_v.at[:, pl.ds(BAND[0], BAND[1] - BAND[0]), :]),
        (inner_w, inner_v),
        (side_w, side_v),
        (marks_h, marks),
        (outer_w, outer_v),
        (cell_y_w, cell_y_v),
    ]
    loads = [pltpu.make_async_copy(*pair, load_sem.at[i]) for i, pair in enumerate(pairs)]
    for load in loads[0:4]:
        load.start()
    main_v[:, 0 : BAND[0], :] = jnp.zeros((2, BAND[0], 256), jnp.bfloat16)
    main_v[:, BAND[1] : 512, :] = jnp.zeros((2, 512 - BAND[1], 256), jnp.bfloat16)

    def take_columns(rows):
        both = jnp.concatenate([rows[:, 0:128], rows[:, TILE_Y - 128 : TILE_Y]], axis=1)
        return lax.dot_general(
            take_v[...], both, (((1,), (1,)), ((), ())), preferred_element_type=jnp.float32
        ).astype(jnp.bfloat16)

    def put_columns(taken):
        left_keep = jnp.where(q == 0, 0.0, 1.0)
        right_keep = jnp.where(q == count_y - 1, 0.0, 1.0)
        line = lax.broadcasted_iota(jnp.int32, (32, 128), 0)
        inside = jnp.where(line < 16, left_keep, right_keep).astype(jnp.bfloat16)
        return lax.dot_general(
            taken, put_v[...] * inside, (((0,), (0,)), ((), ())), preferred_element_type=jnp.float32
        ).astype(jnp.bfloat16)

    for load in loads[0:3]:
        load.wait()
    for load in loads[4:]:
        load.start()
    own = tile[...].reshape(OWN, TILE_Y)
    low_rows, high_rows = [], []
    for first in range(0, PLANES_IN, PACK_PLANES):
        block = own[first * TILE_X : min(first + PACK_PLANES, PLANES_IN) * TILE_X]
        taken = dot(pack_v[:, 0 : block.shape[0]], block)
        rows = min(PACK_ROWS, SIDE_ROWS - first * REACH)
        low_rows.append(taken[0:rows])
        high_rows.append(taken[PACK_ROWS : PACK_ROWS + rows])
    edge_rows = jnp.concatenate(low_rows + high_rows, axis=0).astype(jnp.bfloat16)
    packed[...] = edge_rows
    columns[:, 0:OWN] = take_columns(own)
    for side in range(2):
        corners[side, :, 0:SIDE_ROWS] = take_columns(
            edge_rows[side * SIDE_ROWS : (side + 1) * SIDE_ROWS]
        )

    pl.semaphore_wait(barrier, len(around))
    sends = []
    for i, (dx, dy) in enumerate(around):
        rows, rows_there = (0, SIDE_ROWS) if dx < 0 else (SIDE_ROWS, 0)
        lines, lines_there = (0, 16) if dy < 0 else (16, 0)
        if dx == 0:
            source = columns.at[pl.ds(lines, 16), :]
            target = beside.at[pl.ds(lines_there, 16), :]
        elif dy == 0:
            source = packed.at[pl.ds(rows, SIDE_ROWS), :]
            target = sides.at[pl.ds(rows_there, SIDE_ROWS), :]
        else:
            source = corners.at[rows // SIDE_ROWS, pl.ds(lines, 16), :]
            target = corner_in.at[rows_there // SIDE_ROWS, pl.ds(lines_there, 16), :]
        sends.append(
            pltpu.make_async_remote_copy(
                src_ref=source,
                dst_ref=target,
                send_sem=send_sem.at[i],
                recv_sem=recv_sem.at[i],
                device_id=at(dx, dy),
                device_id_type=MESH,
            )
        )
    for send in sends:
        send.start()
    diagonals = around[4:]
    for dx, dy in diagonals:
        pl.semaphore_signal(far_sem.at[0], inc=1, device_id=at(dx, dy), device_id_type=MESH)

    loads[3].wait()
    for g in range(GROUPS):
        block = tile[g * GROUP_PLANES : g * GROUP_PLANES + GROUP_IN].reshape(
            GROUP_IN * TILE_X, TILE_Y
        )
        smooth[g, :, 128:WIDE_Y] = dot(own_v[0], block) + dot(own_v[1], block)

    for load in loads[4:6]:
        load.wait()
    codes = routing(owner[...], flags[...])
    number = lax.broadcasted_iota(jnp.int32, (count * 8, 256), 0).astype(jnp.float32)
    chosen[...] = jnp.where(number == codes, 1.0, 0.0).astype(jnp.bfloat16)

    pl.semaphore_wait(far_sem.at[0], len(diagonals))
    for dx, dy in diagonals:
        pl.semaphore_signal(
            far_sem.at[1], inc=1, device_id=at(2 * dx, 2 * dy), device_id_type=MESH
        )
    for load in loads[6:]:
        load.wait()
    for send in sends[0:2]:
        send.wait()

    lane = lax.broadcasted_iota(jnp.int32, (1, 128), 1)
    left_out = jnp.where(q == 0, 127, -1)
    right_out = jnp.where(q == count_y - 1, 0, -1)
    edge_keep = jnp.where((lane == left_out) | (lane == right_out), 0.0, 1.0)

    def sigmoid_of(power):
        below = 1.0 + jnp.exp2(jnp.minimum(power, 126.0))
        guess = pl.reciprocal(below, approx=True)
        return guess * (2.0 - below * guess)

    def indicator(blurred):
        high, low = split(blurred)

        def along_y(choose, weights):
            high_part = choose(high)
            return (
                dot(high_part, weights[0])
                + dot(choose(low), weights[0])
                + dot(high_part, weights[1])
            )

        def last(part):
            return jnp.concatenate([part[:, 256:WIDE_Y], part[:, 0:128]], axis=1)

        def right_end(part):
            return jnp.concatenate([part[:, 512:WIDE_Y], part[:, 0:128]], axis=1)

        left = along_y(lambda part: part[:, 0:256], main_v[:, 128:384, 0:128])
        right = along_y(right_end, main_v[:, 128:384, 128:256])
        edge = jnp.where(lane == 127, left, right)
        return split(
            jnp.concatenate(
                [
                    sigmoid_of(along_y(lambda part: part[:, 0:512], main_v[...])),
                    sigmoid_of(along_y(last, main_v[...])),
                    edge_keep * sigmoid_of(edge),
                ],
                axis=1,
            )
        )

    ends[...] = put_columns(beside[:, 0:OWN])
    for g in range(GROUPS):
        first = g * GROUP_PLANES * TILE_X
        block = ends[first : first + GROUP_IN * TILE_X, :]
        smooth[g, :, 0:128] = dot(own_v[0], block) + dot(own_v[1], block)
        high, low = indicator(smooth[g, 0:INNER, :])
        sharp[0, g * INNER : (g + 1) * INNER, :] = high
        sharp[1, g * INNER : (g + 1) * INNER, :] = low
    cells = dot(inner_v[...], sharp[0]) + dot(inner_v[...], sharp[1])

    pl.semaphore_wait(far_sem.at[1], len(diagonals))
    for dx in (-4, 4):
        pl.semaphore_signal(far_sem.at[2], inc=1, device_id=at(dx, 0), device_id_type=MESH)
    for send in sends[2:]:
        send.wait()

    for side in range(2):
        side_ends[side * SIDE_ROWS : (side + 1) * SIDE_ROWS, :] = put_columns(
            corner_in[side, :, 0:SIDE_ROWS]
        )
    low_out = jnp.where(p == 0, 1.0, 0.0)
    high_out = jnp.where(p == count_x - 1, 1.0, 0.0)
    place = lax.broadcasted_iota(jnp.int32, (1, 2 * WINDOW), 1)
    side_keep = jnp.where(place < WINDOW, 1.0 - low_out, 1.0 - high_out).astype(jnp.bfloat16)
    blurred = []
    for g in range(GROUPS):
        low_rows = slice(WINDOW_AT[g], WINDOW_AT[g] + WINDOW)
        high_rows = slice(SIDE_ROWS + WINDOW_AT[g], SIDE_ROWS + WINDOW_AT[g] + WINDOW)
        window = jnp.concatenate(
            [
                jnp.concatenate([side_ends[low_rows, :], sides[low_rows, :]], axis=1),
                jnp.concatenate([side_ends[high_rows, :], sides[high_rows, :]], axis=1),
            ],
            axis=0,
        )
        blurred.append(
            dot(side_v[g, 0] * side_keep, window)
            + dot(side_v[g, 1] * side_keep, window)
            + smooth[g, INNER:GROUP_ROWS, :]
        )
    high, low = indicator(jnp.concatenate(blurred, axis=0))
    keep = (1.0 - low_out * marks[0:1, :] - high_out * marks[1:2, :]).astype(jnp.bfloat16)
    weights = outer_v[...] * keep
    cells = cells + dot(weights, high) + dot(weights, low)

    high, low = split(cells)
    plain = dot(high[0:96], cell_y_v[0]) + dot(low[0:96], cell_y_v[0])
    slopes = dot(high[96:192], cell_y_v[1]) + dot(low[96:192], cell_y_v[1])
    mean_z, mean_x, mean_y = slopes[0:32, 0:128], slopes[32:64, 0:128], slopes[64:96, 128:256]
    shrink = -lax.rsqrt(mean_z * mean_z + mean_x * mean_x + mean_y * mean_y + normal_floor)
    found = [
        plain[0:32, 0:128],
        plain[32:64, 0:128],
        plain[64:96, 0:128],
        plain[0:32, 128:256],
        mean_z * shrink,
        mean_x * shrink,
        mean_y * shrink,
    ]
    for channel in range(CHANNELS):
        geometry[channel] = found[channel]
    write = pltpu.make_async_copy(geometry, geometry_h, geometry_sem)
    write.start()

    most = functools.reduce(jnp.maximum, [jnp.abs(value) for value in found])
    most = jnp.maximum(jnp.max(most, axis=1, keepdims=True), 1e-37)
    grade = jnp.ceil(8.0 * jnp.log2(most) + 0.02)
    stretch = jnp.exp2(grade * -0.125)
    whole = [jnp.floor(value * stretch * LEVELS + 0.5) for value in found]
    whole.append(jnp.broadcast_to(grade, (ROWS, 128)))
    coded = jnp.concatenate(
        [jnp.concatenate(whole[0:4], axis=0), jnp.concatenate(whole[4:8], axis=0)], axis=1
    )
    upper = jnp.floor(coded * (1.0 / 256.0) + 0.5) * 256.0
    stacked[...] = jnp.concatenate([upper, coded - upper], axis=0).astype(jnp.bfloat16)

    def send_to_row(offset, first_step):
        other_p = lax.rem(p + offset, count_x)
        rows = pl.ds(pl.multiple_of(other_p * (count_y * 8), count_y * 8), count_y * 8)
        placed = dot(chosen[rows, :], stacked[...]).astype(jnp.int32)
        joined = (placed[:, 128:256] << 16) | (placed[:, 0:128] & 0xFFFF)
        leaving[pl.ds(other_p * count_y, count_y)] = joined.reshape(count_y, 8, 128)
        for step in range(first_step, count_y):
            other_q = lax.rem(q + step, count_y)
            pltpu.make_async_remote_copy(
                src_ref=leaving.at[other_p * count_y + other_q],
                dst_ref=arrived.at[me],
                send_sem=out_send,
                recv_sem=out_recv,
                device_id=(other_p, other_q),
                device_id_type=MESH,
            ).start()

    def send_rows(offset, carry):
        send_to_row(offset, 0)
        return carry

    send_to_row(0, 1)
    lax.fori_loop(1, 5, send_rows, 0)
    lax.fori_loop(count_x - 4, count_x, send_rows, 0)
    pl.semaphore_wait(far_sem.at[2], 2)
    lax.fori_loop(5, count_x - 4, send_rows, 0)
    stay = pltpu.make_async_copy(leaving.at[me], arrived.at[me], own_sem)
    stay.start()
    others = pl.ds(0, count - 1)
    every = pltpu.make_async_remote_copy(
        src_ref=leaving.at[others],
        dst_ref=arrived.at[others],
        send_sem=out_send,
        recv_sem=out_recv,
        device_id=at(1, 0),
        device_id_type=MESH,
    )
    every.wait_send()
    every.wait_recv()
    stay.wait()
    write.wait()


def decode_kernel(
    coded, geometry_in, received, geometry, received_v, copy_sem, store_sem
):
    pieces = store_sem.shape[0]
    rows = received_v.shape[1] // pieces
    whole = pltpu.make_async_copy(geometry_in, geometry, copy_sem)
    whole.start()
    stores = []
    for i in range(pieces):
        target = pl.ds(i * rows, rows)
        stores.append(
            pltpu.make_async_copy(
                received_v.at[:, target, :], received.at[:, target, :], store_sem.at[i]
            )
        )
    for i in range(pieces):
        target = slice(i * rows, (i + 1) * rows)

        def pair(part):
            both = coded[pl.ds(i * rows * 4 + part, rows, stride=4), :]
            return (both << 16) >> 16, both >> 16

        fourth, grade = pair(3)
        scale = jnp.exp2(grade.astype(jnp.float32) * 0.125) * (1.0 / LEVELS)
        received_v[3, target] = fourth.astype(jnp.float32) * scale
        for part in range(3):
            low, high = pair(part)
            received_v[part, target] = low.astype(jnp.float32) * scale
            received_v[part + 4, target] = high.astype(jnp.float32) * scale
        stores[i].start()
    for store in stores:
        store.wait()
    whole.wait()


def body(count_x, count_y, volume, owner, flags):
    count = count_x * count_y
    inner_w, outer_w = cell_matrices()
    take_w, put_w = column_matrices()
    weights = [
        take_w, pack_matrix(), own_matrix(), along_y_matrix(), put_w, inner_w, side_matrices(), outer_w, cell_y_matrix(),
    ]
    anywhere = pl.BlockSpec(memory_space=pl.ANY)
    bf16 = jnp.bfloat16
    marks = side_marks()
    operands = [volume, owner.reshape(1, ROWS), flags.reshape(1, ROWS), marks, *weights]
    operands = [jnp.asarray(value) for value in operands]
    in_vmem = pl.BlockSpec(memory_space=pltpu.VMEM)
    geometry, arrived = pl.pallas_call(
        functools.partial(kernel, count_x, count_y),
        out_shape=(
            pltpu.VMEM((CHANNELS, ROWS, 128), jnp.float32),
            pltpu.VMEM((count, 8, 128), jnp.int32),
        ),
        in_specs=[anywhere] * (4 + len(weights)),
        out_specs=(anywhere, anywhere),
        scratch_shapes=[
            pltpu.VMEM((PLANES_IN, TILE_X, TILE_Y), bf16),
            pltpu.VMEM((2 * SIDE_ROWS, TILE_Y), bf16),
            pltpu.VMEM((32, 896), bf16),
            pltpu.VMEM((2, 32, 256), bf16),
            pltpu.VMEM((2 * SIDE_ROWS, TILE_Y), bf16),
            pltpu.VMEM((32, 896), bf16),
            pltpu.VMEM((2, 32, 256), bf16),
            pltpu.VMEM((OWN, 128), bf16),
            pltpu.VMEM((2 * SIDE_ROWS, 128), bf16),
            pltpu.VMEM((GROUPS, GROUP_ROWS, WIDE_Y), jnp.float32),
            pltpu.VMEM((2, GROUPS * INNER, WIDE_Y), bf16),
            pltpu.VMEM((count * 8, 256), bf16),
            pltpu.VMEM((256, 256), bf16),
            pltpu.VMEM((count, 8, 128), jnp.int32),
            pltpu.VMEM((CHANNELS, ROWS, 128), jnp.float32),
            pltpu.VMEM((1, ROWS), jnp.int32),
            pltpu.VMEM((1, ROWS), jnp.int32),
            pltpu.VMEM(marks.shape, jnp.float32),
            pltpu.VMEM((2, 512, 256), bf16),
        ]
        + [pltpu.VMEM(weight.shape, bf16) for weight in weights if weight is not weights[3]]
        + [
            pltpu.SemaphoreType.DMA((4 + len(weights),)),
            pltpu.SemaphoreType.DMA((8,)),
            pltpu.SemaphoreType.DMA((8,)),
            pltpu.SemaphoreType.REGULAR((3,)),
            pltpu.SemaphoreType.DMA,
            pltpu.SemaphoreType.DMA,
            pltpu.SemaphoreType.DMA,
            pltpu.SemaphoreType.DMA,
        ],
        compiler_params=pltpu.CompilerParams(
            collective_id=0, has_side_effects=True, vmem_limit_bytes=40 * 2**20
        ),
    )(*[pltpu.with_memory_space_constraint(value, pltpu.HBM) for value in operands])
    pieces = 4
    received, geometry = pl.pallas_call(
        decode_kernel,
        out_shape=(
            jax.ShapeDtypeStruct((CHANNELS, count * 2, 128), jnp.float32),
            jax.ShapeDtypeStruct(geometry.shape, jnp.float32),
        ),
        in_specs=[in_vmem, in_vmem],
        out_specs=(anywhere, anywhere),
        scratch_shapes=[
            pltpu.VMEM((CHANNELS, count * 2, 128), jnp.float32),
            pltpu.SemaphoreType.DMA,
            pltpu.SemaphoreType.DMA((pieces,)),
        ],
        compiler_params=pltpu.CompilerParams(vmem_limit_bytes=16 * 2**20),
    )(arrived.reshape(count * 8, 128), geometry)
    received = jnp.transpose(received, (1, 0, 2))[None]
    return (geometry.reshape(CHANNELS, 4, 8, 128), received)


def solution(mesh):
    in_specs = (P(None, "gx", "gy"), P("gx", "gy", None, None), P("gx", "gy", None))
    out_specs = (P(None, None, "gx", "gy"), P(("gx", "gy"), None, None, None))
    return jax.shard_map(
        functools.partial(body, mesh.shape["gx"], mesh.shape["gy"]),
        mesh=mesh,
        in_specs=in_specs,
        out_specs=out_specs,
        check_vma=False,
    )
```

```python
import functools
import math

import jax
import jax.numpy as jnp
import ml_dtypes
import numpy as np
from jax import lax
from jax.experimental import pallas as pl
from jax.experimental.pallas import tpu as pltpu
from jax.sharding import PartitionSpec as P

MESH = pl.DeviceIdType.MESH

raw_taps = [math.exp(-((offset - 4) ** 2) / 8.0) for offset in range(9)]
gauss_taps = np.array([value / sum(raw_taps) for value in raw_taps])
sharpness = 20.0
normal_floor = 0.01

PLANES_IN = 26
TILE_X = 32
TILE_Y = 512
OWN = PLANES_IN * TILE_X
REACH = 5
WIDE_X = TILE_X + 2
GROUPS = 3
GROUP_PLANES = 6
GROUP_IN = GROUP_PLANES + 8
INNER_X = 24
OUTER_X = 10
INNER = GROUP_PLANES * INNER_X
OUTER = 64
GROUP_ROWS = INNER + OUTER
SIDE_ROWS = 144
WINDOW = 96
WINDOW_AT = [(REACH * GROUP_PLANES * g) // 16 * 16 for g in range(GROUPS)]
PACK_PLANES = 8
PACK_ROWS = PACK_PLANES * REACH
WIDE_Y = TILE_Y + 128
BAND = (112, 400)
ROWS = 32
CHANNELS = 7
LEVELS = 32766.0


def outer_place(x):
    if x < REACH:
        return x
    return x - INNER_X if x >= REACH + INNER_X else None


def row_of(plane, x):
    outer = outer_place(x)
    if outer is None:
        return plane * INNER_X + x - REACH
    return INNER + plane * OUTER_X + outer


def halves(matrix):
    high = matrix.astype(np.float32).astype(ml_dtypes.bfloat16)
    low = (matrix - high.astype(np.float64)).astype(np.float32).astype(ml_dtypes.bfloat16)
    return np.stack([high, low])


def pack_matrix():
    matrix = np.zeros((2 * PACK_ROWS, PACK_PLANES * TILE_X))
    for z in range(PACK_PLANES):
        for i in range(REACH):
            matrix[z * REACH + i, z * TILE_X + i] = 1
            matrix[PACK_ROWS + z * REACH + i, z * TILE_X + TILE_X - REACH + i] = 1
    return matrix.astype(ml_dtypes.bfloat16)


def column_matrices():
    take = np.zeros((32, 256))
    put = np.zeros((32, 128))
    for i in range(REACH):
        take[i, i] = 1
        take[16 + i, 256 - REACH + i] = 1
        put[i, 128 - REACH + i] = 1
        put[16 + i, i] = 1
    return take.astype(ml_dtypes.bfloat16), put.astype(ml_dtypes.bfloat16)


def tap(distance):
    return gauss_taps[distance + 4] if -4 <= distance <= 4 else 0.0


def own_matrix():
    matrix = np.zeros((GROUP_ROWS, GROUP_IN * TILE_X))
    for plane in range(GROUP_PLANES):
        for x in range(WIDE_X):
            for z in range(9):
                for source in range(TILE_X):
                    matrix[row_of(plane, x), (plane + z) * TILE_X + source] = (
                        gauss_taps[z] * tap(source - (x - 1))
                    )
    return halves(matrix)


def side_matrices():
    found = []
    for g in range(GROUPS):
        matrix = np.zeros((OUTER, 2 * WINDOW))
        for plane in range(GROUP_PLANES):
            for x in range(WIDE_X):
                outer = outer_place(x)
                if outer is None:
                    continue
                for z in range(9):
                    for i in range(REACH):
                        row = (g * GROUP_PLANES + plane + z) * REACH + i - WINDOW_AT[g]
                        out = plane * OUTER_X + outer
                        matrix[out, row] = gauss_taps[z] * tap(i - REACH - (x - 1))
                        matrix[out, WINDOW + row] = gauss_taps[z] * tap(TILE_X + i - (x - 1))
        found.append(halves(matrix))
    return np.stack(found)


def along_y_matrix():
    scale = -sharpness / math.log(2.0)
    main = np.zeros((512, 256))
    for out in range(256):
        for distance in range(-4, 5):
            main[128 + out + distance, out] = scale * tap(distance)
    return halves(main)[:, BAND[0] : BAND[1]]


MEAN = np.array([0, 1, 1, 1, 1, 0]) / 4
FIRST = np.array([0, 1, 0, 0, 0, 0]) / 1
SOFT = np.array([1, 3, 4, 4, 3, 1]) / 16
SLOPE = np.array([-1, -1, 0, 0, 1, 1]) / 8


def cell_matrices():
    pairs = [(MEAN, MEAN), (FIRST, MEAN), (MEAN, FIRST), (SLOPE, SOFT), (SOFT, SLOPE), (SOFT, SOFT)]
    inner = np.zeros((len(pairs) * ROWS, GROUPS * INNER))
    outer = np.zeros((len(pairs) * ROWS, GROUPS * OUTER))
    for at, (along_z, along_x) in enumerate(pairs):
        for layer in range(4):
            for cell in range(8):
                for z in range(6):
                    for x in range(6):
                        group, plane = divmod(4 * layer + z, GROUP_PLANES)
                        row = row_of(plane, 4 * cell + x)
                        out = at * ROWS + layer * 8 + cell
                        weight = along_z[z] * along_x[x]
                        if row < INNER:
                            inner[out, group * INNER + row] += weight
                        else:
                            outer[out, group * OUTER + row - INNER] += weight
    return inner.astype(ml_dtypes.bfloat16), outer.astype(ml_dtypes.bfloat16)


def cell_y_matrix():
    matrix = np.zeros((2, TILE_Y + 128, 256))
    for at, weights in enumerate((MEAN, FIRST, SOFT, SLOPE)):
        for cell in range(128):
            for y in range(6):
                place = 4 * cell + y - 1
                row = TILE_Y + 127 if place < 0 else place
                matrix[at // 2, row, at % 2 * 128 + cell] = weights[y]
    return matrix.astype(ml_dtypes.bfloat16)


def side_marks():
    marks = np.zeros((8, GROUPS * OUTER), np.float32)
    for group in range(GROUPS):
        for plane in range(GROUP_PLANES):
            marks[0, group * OUTER + plane * OUTER_X] = 1
            marks[1, group * OUTER + plane * OUTER_X + OUTER_X - 1] = 1
    return marks


def split(value):
    high = value.astype(jnp.bfloat16)
    return high, (value - high.astype(jnp.float32)).astype(jnp.bfloat16)


def dot(left, right):
    return jnp.dot(left, right, preferred_element_type=jnp.float32)


def routing(owner, flags):
    wide = (ROWS, ROWS)
    row = lax.broadcasted_iota(jnp.int32, wide, 0)
    column = lax.broadcasted_iota(jnp.int32, wide, 1)
    owner_across = jnp.broadcast_to(owner.astype(jnp.float32), wide)
    flag_across = jnp.broadcast_to(flags.astype(jnp.float32), wide)
    same = row == column
    owner_down = jnp.sum(jnp.where(same, owner_across, 0.0), axis=1, keepdims=True)
    flag_down = jnp.sum(jnp.where(same, flag_across, 0.0), axis=1, keepdims=True)
    earlier = (column < row) & (owner_down == owner_across)
    slot = jnp.sum(jnp.where(earlier, flag_across, 0.0), axis=1, keepdims=True)
    code = jnp.where(flag_down > 0.5, owner_down * 2.0 + slot, -8.0)
    place = lax.broadcasted_iota(jnp.int32, (ROWS, 256), 1)
    mine = (place & (ROWS - 1)) == lax.broadcasted_iota(jnp.int32, (ROWS, 256), 0)
    spread = jnp.sum(jnp.where(mine, code, 0.0), axis=0, keepdims=True)
    part = ((lax.broadcasted_iota(jnp.int32, (1, 256), 1) >> 5) & 3).astype(jnp.float32)
    return spread * 4.0 + part


def kernel(
    count_x, count_y,
    volume, owner_h, flags_h, marks_h,
    take_w, pack_w, own_w, main_w, put_w, inner_w, side_w, outer_w, cell_y_w,
    geometry_h, arrived,
    tile, packed, columns, corners, sides, beside, corner_in, ends, side_ends,
    smooth, sharp, chosen, stacked, leaving, geometry, owner, flags, marks, main_v,
    take_v, pack_v, own_v, put_v, inner_v, side_v, outer_v, cell_y_v,
    load_sem, send_sem, recv_sem, far_sem, out_send, out_recv, own_sem, geometry_sem,
):
    p = lax.axis_index("gx")
    q = lax.axis_index("gy")
    count = count_x * count_y
    me = p * count_y + q

    def at(dx, dy):
        return (lax.rem(p + dx + count_x, count_x), lax.rem(q + dy + count_y, count_y))

    around = [(0, -1), (0, 1), (-1, 0), (1, 0), (-1, -1), (-1, 1), (1, -1), (1, 1)]
    barrier = pltpu.get_barrier_semaphore()
    pairs = [
        (volume, tile),
        (pack_w, pack_v),
        (take_w, take_v),
        (own_w, own_v),
        (owner_h, owner),
        (flags_h, flags),
        (put_w, put_v),
        (main_w, main_v.at[:, pl.ds(BAND[0], BAND[1] - BAND[0]), :]),
        (inner_w, inner_v),
        (side_w, side_v),
        (marks_h, marks),
        (outer_w, outer_v),
        (cell_y_w, cell_y_v),
    ]
    loads = [pltpu.make_async_copy(*pair, load_sem.at[i]) for i, pair in enumerate(pairs)]
    loads[0].start()
    for dx, dy in around:
        pl.semaphore_signal(barrier, inc=1, device_id=at(dx, dy), device_id_type=MESH)
    for load in loads[1:4]:
        load.start()
    main_v[:, 0 : BAND[0], :] = jnp.zeros((2, BAND[0], 256), jnp.bfloat16)
    main_v[:, BAND[1] : 512, :] = jnp.zeros((2, 512 - BAND[1], 256), jnp.bfloat16)

    def take_columns(rows):
        both = jnp.concatenate([rows[:, 0:128], rows[:, TILE_Y - 128 : TILE_Y]], axis=1)
        return lax.dot_general(
            take_v[...], both, (((1,), (1,)), ((), ())), preferred_element_type=jnp.float32
        ).astype(jnp.bfloat16)

    def put_columns(taken):
        left_keep = jnp.where(q == 0, 0.0, 1.0)
        right_keep = jnp.where(q == count_y - 1, 0.0, 1.0)
        line = lax.broadcasted_iota(jnp.int32, (32, 128), 0)
        inside = jnp.where(line < 16, left_keep, right_keep).astype(jnp.bfloat16)
        return lax.dot_general(
            taken, put_v[...] * inside, (((0,), (0,)), ((), ())), preferred_element_type=jnp.float32
        ).astype(jnp.bfloat16)

    for load in loads[0:3]:
        load.wait()
    for load in loads[4:]:
        load.start()
    own = tile[...].reshape(OWN, TILE_Y)
    low_rows, high_rows = [], []
    for first in range(0, PLANES_IN, PACK_PLANES):
        block = own[first * TILE_X : min(first + PACK_PLANES, PLANES_IN) * TILE_X]
        taken = dot(pack_v[:, 0 : block.shape[0]], block)
        rows = min(PACK_ROWS, SIDE_ROWS - first * REACH)
        low_rows.append(taken[0:rows])
        high_rows.append(taken[PACK_ROWS : PACK_ROWS + rows])
    edge_rows = jnp.concatenate(low_rows + high_rows, axis=0).astype(jnp.bfloat16)
    packed[...] = edge_rows
    columns[:, 0:OWN] = take_columns(own)
    for side in range(2):
        corners[side, :, 0:SIDE_ROWS] = take_columns(
            edge_rows[side * SIDE_ROWS : (side + 1) * SIDE_ROWS]
        )

    pl.semaphore_wait(barrier, len(around))
    sends = []
    for i, (dx, dy) in enumerate(around):
        rows, rows_there = (0, SIDE_ROWS) if dx < 0 else (SIDE_ROWS, 0)
        lines, lines_there = (0, 16) if dy < 0 else (16, 0)
        if dx == 0:
            source = columns.at[pl.ds(lines, 16), :]
            target = beside.at[pl.ds(lines_there, 16), :]
        elif dy == 0:
            source = packed.at[pl.ds(rows, SIDE_ROWS), :]
            target = sides.at[pl.ds(rows_there, SIDE_ROWS), :]
        else:
            source = corners.at[rows // SIDE_ROWS, pl.ds(lines, 16), :]
            target = corner_in.at[rows_there // SIDE_ROWS, pl.ds(lines_there, 16), :]
        sends.append(
            pltpu.make_async_remote_copy(
                src_ref=source,
                dst_ref=target,
                send_sem=send_sem.at[i],
                recv_sem=recv_sem.at[i],
                device_id=at(dx, dy),
                device_id_type=MESH,
            )
        )
    for send in sends:
        send.start()
    diagonals = around[4:]
    for dx, dy in diagonals:
        pl.semaphore_signal(far_sem.at[0], inc=1, device_id=at(dx, dy), device_id_type=MESH)

    loads[3].wait()
    for g in range(GROUPS):
        block = tile[g * GROUP_PLANES : g * GROUP_PLANES + GROUP_IN].reshape(
            GROUP_IN * TILE_X, TILE_Y
        )
        smooth[g, :, 128:WIDE_Y] = dot(own_v[0], block) + dot(own_v[1], block)

    for load in loads[4:6]:
        load.wait()
    codes = routing(owner[...], flags[...])
    number = lax.broadcasted_iota(jnp.int32, (count * 8, 256), 0).astype(jnp.float32)
    chosen[...] = jnp.where(number == codes, 1.0, 0.0).astype(jnp.bfloat16)

    pl.semaphore_wait(far_sem.at[0], len(diagonals))
    for dx, dy in diagonals:
        pl.semaphore_signal(
            far_sem.at[1], inc=1, device_id=at(2 * dx, 2 * dy), device_id_type=MESH
        )
    for load in loads[6:]:
        load.wait()
    for send in sends[0:2]:
        send.wait()

    lane = lax.broadcasted_iota(jnp.int32, (1, 128), 1)
    left_out = jnp.where(q == 0, 127, -1)
    right_out = jnp.where(q == count_y - 1, 0, -1)
    edge_keep = jnp.where((lane == left_out) | (lane == right_out), 0.0, 1.0)

    def sigmoid_of(power):
        below = 1.0 + jnp.exp2(jnp.minimum(power, 126.0))
        guess = pl.reciprocal(below, approx=True)
        return guess * (2.0 - below * guess)

    def indicator(blurred):
        high, low = split(blurred)

        def along_y(choose, weights):
            high_part = choose(high)
            return (
                dot(high_part, weights[0])
                + dot(choose(low), weights[0])
                + dot(high_part, weights[1])
            )

        def last(part):
            return jnp.concatenate([part[:, 256:WIDE_Y], part[:, 0:128]], axis=1)

        def right_end(part):
            return jnp.concatenate([part[:, 512:WIDE_Y], part[:, 0:128]], axis=1)

        left = along_y(lambda part: part[:, 0:256], main_v[:, 128:384, 0:128])
        right = along_y(right_end, main_v[:, 128:384, 128:256])
        edge = jnp.where(lane == 127, left, right)
        return split(
            jnp.concatenate(
                [
                    sigmoid_of(along_y(lambda part: part[:, 0:512], main_v[...])),
                    sigmoid_of(along_y(last, main_v[...])),
                    edge_keep * sigmoid_of(edge),
                ],
                axis=1,
            )
        )

    ends[...] = put_columns(beside[:, 0:OWN])
    for g in range(GROUPS):
        first = g * GROUP_PLANES * TILE_X
        block = ends[first : first + GROUP_IN * TILE_X, :]
        smooth[g, :, 0:128] = dot(own_v[0], block) + dot(own_v[1], block)
        high, low = indicator(smooth[g, 0:INNER, :])
        sharp[0, g * INNER : (g + 1) * INNER, :] = high
        sharp[1, g * INNER : (g + 1) * INNER, :] = low
    cells = dot(inner_v[...], sharp[0]) + dot(inner_v[...], sharp[1])

    pl.semaphore_wait(far_sem.at[1], len(diagonals))
    for dx in (-4, 4):
        pl.semaphore_signal(far_sem.at[2], inc=1, device_id=at(dx, 0), device_id_type=MESH)
    for send in sends[2:]:
        send.wait()

    for side in range(2):
        side_ends[side * SIDE_ROWS : (side + 1) * SIDE_ROWS, :] = put_columns(
            corner_in[side, :, 0:SIDE_ROWS]
        )
    low_out = jnp.where(p == 0, 1.0, 0.0)
    high_out = jnp.where(p == count_x - 1, 1.0, 0.0)
    place = lax.broadcasted_iota(jnp.int32, (1, 2 * WINDOW), 1)
    side_keep = jnp.where(place < WINDOW, 1.0 - low_out, 1.0 - high_out).astype(jnp.bfloat16)
    blurred = []
    for g in range(GROUPS):
        low_rows = slice(WINDOW_AT[g], WINDOW_AT[g] + WINDOW)
        high_rows = slice(SIDE_ROWS + WINDOW_AT[g], SIDE_ROWS + WINDOW_AT[g] + WINDOW)
        window = jnp.concatenate(
            [
                jnp.concatenate([side_ends[low_rows, :], sides[low_rows, :]], axis=1),
                jnp.concatenate([side_ends[high_rows, :], sides[high_rows, :]], axis=1),
            ],
            axis=0,
        )
        blurred.append(
            dot(side_v[g, 0] * side_keep, window)
            + dot(side_v[g, 1] * side_keep, window)
            + smooth[g, INNER:GROUP_ROWS, :]
        )
    high, low = indicator(jnp.concatenate(blurred, axis=0))
    keep = (1.0 - low_out * marks[0:1, :] - high_out * marks[1:2, :]).astype(jnp.bfloat16)
    weights = outer_v[...] * keep
    cells = cells + dot(weights, high) + dot(weights, low)

    high, low = split(cells)
    plain = dot(high[0:96], cell_y_v[0]) + dot(low[0:96], cell_y_v[0])
    slopes = dot(high[96:192], cell_y_v[1]) + dot(low[96:192], cell_y_v[1])
    mean_z, mean_x, mean_y = slopes[0:32, 0:128], slopes[32:64, 0:128], slopes[64:96, 128:256]
    shrink = -lax.rsqrt(mean_z * mean_z + mean_x * mean_x + mean_y * mean_y + normal_floor)
    found = [
        plain[0:32, 0:128],
        plain[32:64, 0:128],
        plain[64:96, 0:128],
        plain[0:32, 128:256],
        mean_z * shrink,
        mean_x * shrink,
        mean_y * shrink,
    ]
    for channel in range(CHANNELS):
        geometry[channel] = found[channel]
    write = pltpu.make_async_copy(geometry, geometry_h, geometry_sem)
    write.start()

    most = functools.reduce(jnp.maximum, [jnp.abs(value) for value in found])
    most = jnp.maximum(jnp.max(most, axis=1, keepdims=True), 1e-37)
    grade = jnp.ceil(8.0 * jnp.log2(most) + 0.02)
    stretch = jnp.exp2(grade * -0.125)
    whole = [jnp.floor(value * stretch * LEVELS + 0.5) for value in found]
    whole.append(jnp.broadcast_to(grade, (ROWS, 128)))
    coded = jnp.concatenate(
        [jnp.concatenate(whole[0:4], axis=0), jnp.concatenate(whole[4:8], axis=0)], axis=1
    )
    upper = jnp.floor(coded * (1.0 / 256.0) + 0.5) * 256.0
    stacked[...] = jnp.concatenate([upper, coded - upper], axis=0).astype(jnp.bfloat16)

    def send_to_row(offset, first_step):
        other_p = lax.rem(p + offset, count_x)
        rows = pl.ds(pl.multiple_of(other_p * (count_y * 8), count_y * 8), count_y * 8)
        placed = dot(chosen[rows, :], stacked[...]).astype(jnp.int32)
        joined = (placed[:, 128:256] << 16) | (placed[:, 0:128] & 0xFFFF)
        leaving[pl.ds(other_p * count_y, count_y)] = joined.reshape(count_y, 8, 128)
        for step in range(first_step, count_y):
            other_q = lax.rem(q + step, count_y)
            pltpu.make_async_remote_copy(
                src_ref=leaving.at[other_p * count_y + other_q],
                dst_ref=arrived.at[me],
                send_sem=out_send,
                recv_sem=out_recv,
                device_id=(other_p, other_q),
                device_id_type=MESH,
            ).start()

    def send_rows(offset, carry):
        send_to_row(offset, 0)
        return carry

    send_to_row(0, 1)
    lax.fori_loop(1, 5, send_rows, 0)
    lax.fori_loop(count_x - 4, count_x, send_rows, 0)
    pl.semaphore_wait(far_sem.at[2], 2)
    lax.fori_loop(5, count_x - 4, send_rows, 0)
    stay = pltpu.make_async_copy(leaving.at[me], arrived.at[me], own_sem)
    stay.start()
    others = pl.ds(0, count - 1)
    every = pltpu.make_async_remote_copy(
        src_ref=leaving.at[others],
        dst_ref=arrived.at[others],
        send_sem=out_send,
        recv_sem=out_recv,
        device_id=at(1, 0),
        device_id_type=MESH,
    )
    every.wait_send()
    every.wait_recv()
    stay.wait()
    write.wait()


def decode_kernel(
    coded, geometry_in, received, geometry, received_v, copy_sem, store_sem
):
    pieces = store_sem.shape[0]
    rows = received_v.shape[1] // pieces
    whole = pltpu.make_async_copy(geometry_in, geometry, copy_sem)
    whole.start()
    stores = []
    for i in range(pieces):
        target = pl.ds(i * rows, rows)
        stores.append(
            pltpu.make_async_copy(
                received_v.at[:, target, :], received.at[:, target, :], store_sem.at[i]
            )
        )
    for i in range(pieces):
        target = slice(i * rows, (i + 1) * rows)

        def pair(part):
            both = coded[pl.ds(i * rows * 4 + part, rows, stride=4), :]
            return (both << 16) >> 16, both >> 16

        fourth, grade = pair(3)
        scale = jnp.exp2(grade.astype(jnp.float32) * 0.125) * (1.0 / LEVELS)
        received_v[3, target] = fourth.astype(jnp.float32) * scale
        for part in range(3):
            low, high = pair(part)
            received_v[part, target] = low.astype(jnp.float32) * scale
            received_v[part + 4, target] = high.astype(jnp.float32) * scale
        stores[i].start()
    for store in stores:
        store.wait()
    whole.wait()


def body(count_x, count_y, volume, owner, flags):
    count = count_x * count_y
    inner_w, outer_w = cell_matrices()
    take_w, put_w = column_matrices()
    weights = [
        take_w, pack_matrix(), own_matrix(), along_y_matrix(), put_w, inner_w, side_matrices(), outer_w, cell_y_matrix(),
    ]
    anywhere = pl.BlockSpec(memory_space=pl.ANY)
    bf16 = jnp.bfloat16
    marks = side_marks()
    operands = [volume, owner.reshape(1, ROWS), flags.reshape(1, ROWS), marks, *weights]
    operands = [jnp.asarray(value) for value in operands]
    in_vmem = pl.BlockSpec(memory_space=pltpu.VMEM)
    geometry, arrived = pl.pallas_call(
        functools.partial(kernel, count_x, count_y),
        out_shape=(
            pltpu.VMEM((CHANNELS, ROWS, 128), jnp.float32),
            pltpu.VMEM((count, 8, 128), jnp.int32),
        ),
        in_specs=[anywhere] * (4 + len(weights)),
        out_specs=(anywhere, anywhere),
        scratch_shapes=[
            pltpu.VMEM((PLANES_IN, TILE_X, TILE_Y), bf16),
            pltpu.VMEM((2 * SIDE_ROWS, TILE_Y), bf16),
            pltpu.VMEM((32, 896), bf16),
            pltpu.VMEM((2, 32, 256), bf16),
            pltpu.VMEM((2 * SIDE_ROWS, TILE_Y), bf16),
            pltpu.VMEM((32, 896), bf16),
            pltpu.VMEM((2, 32, 256), bf16),
            pltpu.VMEM((OWN, 128), bf16),
            pltpu.VMEM((2 * SIDE_ROWS, 128), bf16),
            pltpu.VMEM((GROUPS, GROUP_ROWS, WIDE_Y), jnp.float32),
            pltpu.VMEM((2, GROUPS * INNER, WIDE_Y), bf16),
            pltpu.VMEM((count * 8, 256), bf16),
            pltpu.VMEM((256, 256), bf16),
            pltpu.VMEM((count, 8, 128), jnp.int32),
            pltpu.VMEM((CHANNELS, ROWS, 128), jnp.float32),
            pltpu.VMEM((1, ROWS), jnp.int32),
            pltpu.VMEM((1, ROWS), jnp.int32),
            pltpu.VMEM(marks.shape, jnp.float32),
            pltpu.VMEM((2, 512, 256), bf16),
        ]
        + [pltpu.VMEM(weight.shape, bf16) for weight in weights if weight is not weights[3]]
        + [
            pltpu.SemaphoreType.DMA((4 + len(weights),)),
            pltpu.SemaphoreType.DMA((8,)),
            pltpu.SemaphoreType.DMA((8,)),
            pltpu.SemaphoreType.REGULAR((3,)),
            pltpu.SemaphoreType.DMA,
            pltpu.SemaphoreType.DMA,
            pltpu.SemaphoreType.DMA,
            pltpu.SemaphoreType.DMA,
        ],
        compiler_params=pltpu.CompilerParams(
            collective_id=0, has_side_effects=True, vmem_limit_bytes=40 * 2**20
        ),
    )(*[pltpu.with_memory_space_constraint(value, pltpu.HBM) for value in operands])
    pieces = 4
    received, geometry = pl.pallas_call(
        decode_kernel,
        out_shape=(
            jax.ShapeDtypeStruct((CHANNELS, count * 2, 128), jnp.float32),
            jax.ShapeDtypeStruct(geometry.shape, jnp.float32),
        ),
        in_specs=[in_vmem, in_vmem],
        out_specs=(anywhere, anywhere),
        scratch_shapes=[
            pltpu.VMEM((CHANNELS, count * 2, 128), jnp.float32),
            pltpu.SemaphoreType.DMA,
            pltpu.SemaphoreType.DMA((pieces,)),
        ],
        compiler_params=pltpu.CompilerParams(vmem_limit_bytes=16 * 2**20),
    )(arrived.reshape(count * 8, 128), geometry)
    received = jnp.transpose(received, (1, 0, 2))[None]
    return (geometry.reshape(CHANNELS, 4, 8, 128), received)


def solution(mesh):
    in_specs = (P(None, "gx", "gy"), P("gx", "gy", None, None), P("gx", "gy", None))
    out_specs = (P(None, None, "gx", "gy"), P(("gx", "gy"), None, None, None))
    return jax.shard_map(
        functools.partial(body, mesh.shape["gx"], mesh.shape["gy"]),
        mesh=mesh,
        in_specs=in_specs,
        out_specs=out_specs,
        check_vma=False,
    )
```
